512 devices in a mesh: blk: 512 (over z, y, x, core).
Axes of the slice: x: 4, y: 8, z: 8, core: 2. Of those that a mesh axis runs over, the one named last changes fastest.
Arguments:
- populations: float32 [16384, 19, 512], P('blk'), may hold values from 0 to 1, as said below
- coarse_faces: float32 [1024, 2, 19, 64], P('blk'), may hold values from 0 to 1, as said below
- neighbors: int32 [16384, 6], P('blk'), may hold values from -1 to 16383, as said below
- interface: int32 [16384, 2], P('blk'), may hold values from -1 to 1023, as said below
- solid: int32 [16384, 512], P('blk'), may hold values from 0 to 1, as said below
Outputs:
- advanced: float32 [16384, 19, 512], P('blk')
The draws below stay inside these ranges and needn't reach their ends.
Inputs may be any that keep to these rules, and one draw needn't show every extreme that they name: `populations`: every entry is positive. `coarse_faces`: every entry is positive. `neighbors`: Symmetric: a is across face d of b exactly when b is across the opposite face of a. Blocks b with equal b // 32 share an owner. A block across a y or z face has the same owner; one across the +x (-x) face has the same owner or the next (previous) one. For each owner and each x direction at most 16 of its blocks have a neighbour with another owner, and some owner reaches 16 in each direction. The +y face of a block with interface[b, 0] >= 0 is -1 here. interface[b, 0] is owned by the next owner: interface[b, 0] // 2 == b // 32 + 1. interface[b, 1] is the quadrant, 0 to 3. Each pair of coarse block and quadrant appears at most once. `solid`: only cells with all three coordinates in 1..6 are wall cells.
All inputs are finite; a program needn't handle non-finite values.
Results may differ from the reference program's by a relative error of at most 0.0001.
Values sent between devices are 32-bit elements; how exact they have to be, the bound alone decides.
A program may use at most 64 MiB of HBM per device.

```python
import jax
import jax.numpy as jnp
import numpy as np
from jax import lax

SIDE = 4
CROSS = 16
SLICES_DEV = 2
Q = 19
CELLS = 512
FACE = 64
BLK_DEV = 32
CB_DEV = 2
BLOCKS = 16384
CBLOCKS = 1024
N_BLK = 512


velocity_draw = np.array([[0, 0, 0], [1, 0, 0], [-1, 0, 0], [0, 1, 0], [0, -1, 0], [0, 0, 1], [0, 0, -1], [1, 1, 0], [-1, -1, 0], [1, -1, 0], [-1, 1, 0], [1, 0, 1], [-1, 0, -1], [1, 0, -1], [-1, 0, 1], [0, 1, 1], [0, -1, -1], [0, 1, -1], [0, -1, 1]], dtype=np.float32)


weight_draw = np.array([1.0 / 3.0] + [1.0 / 18.0] * 6 + [1.0 / 36.0] * 12, dtype=np.float32)


def near_state(key, leading, cells):
    key_rho, key_vel, key_noise = jax.random.split(key, 3)
    density = 1.0 + 0.1 * jax.random.uniform(key_rho, (leading, 1, cells), jnp.float32, -1.0, 1.0)
    velocity = 0.04 * jnp.clip(jax.random.normal(key_vel, (leading, 3, cells), jnp.float32), -2.5, 2.5)
    noise = 0.3 * jax.random.uniform(key_noise, (leading, 19, cells), jnp.float32, -1.0, 1.0)
    vel_table = jnp.asarray(velocity_draw)
    project = vel_table[None, :, 0:1] * velocity[:, 0:1, :] + vel_table[None, :, 1:2] * velocity[:, 1:2, :] + vel_table[None, :, 2:3] * velocity[:, 2:3, :]
    square = jnp.sum(velocity * velocity, axis=1, keepdims=True)
    balance = jnp.asarray(weight_draw)[None, :, None] * density * (1.0 + 3.0 * project + 4.5 * project * project - 1.5 * square)
    return balance * (1.0 + noise)


def draw_populations(key, part):
    return near_state(jax.random.fold_in(key, 21), BLOCKS, CELLS)


def draw_coarse_faces(key, part):
    start_state = near_state(jax.random.fold_in(key, 22), CBLOCKS, FACE)
    end_state = near_state(jax.random.fold_in(key, 23), CBLOCKS, FACE)
    return jnp.stack([start_state, end_state], axis=1)


def behind(keep, step):
    return jnp.concatenate([jnp.zeros((step,), dtype=bool), keep[:-step]])


def geometry(key):
    owners = BLOCKS // BLK_DEV
    positions = jnp.arange(BLOCKS, dtype=jnp.int32)
    device_of = positions // BLK_DEV
    local_pos = positions % BLK_DEV
    slice_of = local_pos // CROSS
    cross_y = local_pos % CROSS // SIDE
    cross_z = local_pos % SIDE
    shuffles = jax.vmap(lambda sub_key: jax.random.permutation(sub_key, BLK_DEV))(jax.random.split(jax.random.fold_in(key, 11), owners))
    block_id = device_of * BLK_DEV + shuffles.reshape(-1).astype(jnp.int32)
    keep_x = jax.random.randint(jax.random.fold_in(key, 12), (BLOCKS,), 0, 8) != 0
    forced_owner = jax.random.randint(jax.random.fold_in(key, 13), (), 0, owners - 1)
    keep_x = (keep_x | (device_of == forced_owner) & (slice_of == SLICES_DEV - 1)) & (positions + CROSS < BLOCKS)
    keep_y = (jax.random.randint(jax.random.fold_in(key, 14), (BLOCKS,), 0, 8) != 0) & (cross_y < SIDE - 1)
    keep_z = (jax.random.randint(jax.random.fold_in(key, 15), (BLOCKS,), 0, 8) != 0) & (cross_z < SIDE - 1)
    plus_x = jnp.where(keep_x, positions + CROSS, -1)
    minus_x = jnp.where(behind(keep_x, CROSS), positions - CROSS, -1)
    plus_y = jnp.where(keep_y, positions + SIDE, -1)
    minus_y = jnp.where(behind(keep_y, SIDE), positions - SIDE, -1)
    plus_z = jnp.where(keep_z, positions + 1, -1)
    minus_z = jnp.where(behind(keep_z, 1), positions - 1, -1)
    by_pos = jnp.stack([plus_x, minus_x, plus_y, minus_y, plus_z, minus_z], axis=1)
    as_ids = jnp.where(by_pos >= 0, block_id[jnp.clip(by_pos, 0, BLOCKS - 1)], -1)
    neighbor_table = jnp.zeros((BLOCKS, 6), jnp.int32).at[block_id].set(as_ids.astype(jnp.int32))
    coarse_shuffle = jax.vmap(lambda sub_key: jax.random.permutation(sub_key, CB_DEV))(jax.random.split(jax.random.fold_in(key, 16), owners))
    coarse_local = slice_of // 2 * (SIDE // 2) + cross_z // 2
    upper_owner = jnp.minimum(device_of + 1, owners - 1)
    coarse_id = upper_owner * CB_DEV + coarse_shuffle[upper_owner, coarse_local].astype(jnp.int32)
    quadrant = 2 * (slice_of % 2) + cross_z % 2
    linked = (jax.random.randint(jax.random.fold_in(key, 17), (BLOCKS,), 0, 4) != 0) | (quadrant == 0)
    has_link = (cross_y == SIDE - 1) & linked & (device_of < owners - 1)
    link_pos = jnp.stack([jnp.where(has_link, coarse_id, -1), quadrant], axis=1).astype(jnp.int32)
    interface_table = jnp.zeros((BLOCKS, 2), jnp.int32).at[block_id].set(link_pos)
    return (neighbor_table, interface_table)


def draw_neighbors(key, part):
    return geometry(key)[0]


def draw_interface(key, part):
    return geometry(key)[1]


def draw_solid(key, part):
    cells = jnp.arange(CELLS, dtype=jnp.int32)
    coord_i = cells // 64
    coord_j = cells // 8 % 8
    coord_k = cells % 8
    inner = (coord_i >= 1) & (coord_i <= 6) & (coord_j >= 1) & (coord_j <= 6) & (coord_k >= 1) & (coord_k <= 6)
    marks = jax.random.randint(jax.random.fold_in(key, 31), (BLOCKS, CELLS), 0, 16) == 0
    return (marks & inner[None, :]).astype(jnp.int32)


def setup_inputs(seed: int = 0) -> dict:
    keys = jax.random.split(jax.random.key(seed), 6)
    return {
        "populations": draw_populations(jax.random.fold_in(keys[5], 71), 0),
        "coarse_faces": draw_coarse_faces(jax.random.fold_in(keys[5], 71), 0),
        "neighbors": draw_neighbors(jax.random.fold_in(keys[5], 71), 0),
        "interface": draw_interface(jax.random.fold_in(keys[5], 71), 0),
        "solid": draw_solid(jax.random.fold_in(keys[5], 71), 0),
    }


def velocity_list():
    return [[0, 0, 0], [1, 0, 0], [-1, 0, 0], [0, 1, 0], [0, -1, 0], [0, 0, 1], [0, 0, -1],
            [1, 1, 0], [-1, -1, 0], [1, -1, 0], [-1, 1, 0], [1, 0, 1], [-1, 0, -1], [1, 0, -1],
            [-1, 0, 1], [0, 1, 1], [0, -1, -1], [0, 1, -1], [0, -1, 1]]


def opposite_list():
    return [0, 2, 1, 4, 3, 6, 5, 8, 7, 10, 9, 12, 11, 14, 13, 16, 15, 18, 17]


def build_relax():
    velocity_set = np.array(velocity_list())
    shear_rate = 1.0 / 0.6
    vel_x = velocity_set[:, 0] * 1.0
    vel_y = velocity_set[:, 1] * 1.0
    vel_z = velocity_set[:, 2] * 1.0
    speed_sq = vel_x * vel_x + vel_y * vel_y + vel_z * vel_z
    moment_rows = [np.ones(19), 19.0 * speed_sq - 30.0, (21.0 * speed_sq * speed_sq - 53.0 * speed_sq + 24.0) / 2.0,
                   vel_x, (5.0 * speed_sq - 9.0) * vel_x, vel_y, (5.0 * speed_sq - 9.0) * vel_y,
                   vel_z, (5.0 * speed_sq - 9.0) * vel_z, 3.0 * vel_x * vel_x - speed_sq,
                   (3.0 * speed_sq - 5.0) * (3.0 * vel_x * vel_x - speed_sq), vel_y * vel_y - vel_z * vel_z,
                   (3.0 * speed_sq - 5.0) * (vel_y * vel_y - vel_z * vel_z), vel_x * vel_y, vel_y * vel_z,
                   vel_x * vel_z, (vel_y * vel_y - vel_z * vel_z) * vel_x, (vel_z * vel_z - vel_x * vel_x) * vel_y,
                   (vel_x * vel_x - vel_y * vel_y) * vel_z]
    moments = np.stack(moment_rows)
    relax_rates = np.array([0.0, 1.19, 1.4, 0.0, 1.2, 0.0, 1.2, 0.0, 1.2, shear_rate, 1.4, shear_rate, 1.4,
                            shear_rate, shear_rate, shear_rate, 1.98, 1.98, 1.98])
    row_norms = np.sum(moments * moments, axis=1)
    return moments.T @ ((relax_rates / row_norms)[:, None] * moments)


def build_crossing():
    velocity_set = velocity_list()
    crossing_list = []
    for face_dir in range(6):
        axis_pos = face_dir // 2
        sign_val = 1 if face_dir % 2 == 0 else -1
        members = [lattice_dir for lattice_dir in range(19) if velocity_set[lattice_dir][axis_pos] == -sign_val]
        crossing_list.append(members)
    return crossing_list


def build_layers():
    layer_list = []
    for face_dir in range(6):
        axis_pos = face_dir // 2
        level = 7 if face_dir % 2 == 0 else 0
        others = [other_axis for other_axis in range(3) if other_axis != axis_pos]
        cell_list = []
        for first_coord in range(8):
            for second_coord in range(8):
                coords = [0, 0, 0]
                coords[axis_pos] = level
                coords[others[0]] = first_coord
                coords[others[1]] = second_coord
                cell_list.append(64 * coords[0] + 8 * coords[1] + coords[2])
        layer_list.append(np.array(cell_list, dtype=np.int32))
    return layer_list


def build_sources():
    velocity_set = velocity_list()
    side_table = np.full((19, 512), -1, dtype=np.int32)
    ghost_table = np.zeros((19, 512), dtype=np.int32)
    for lattice_dir in range(19):
        for cell in range(512):
            coords = [cell // 64, (cell // 8) % 8, cell % 8]
            source = [coords[axis_pos] - velocity_set[lattice_dir][axis_pos] for axis_pos in range(3)]
            outside = [axis_pos for axis_pos in range(3) if source[axis_pos] < 0 or source[axis_pos] > 7]
            if len(outside) == 1:
                axis_pos = outside[0]
                side_table[lattice_dir, cell] = 2 * axis_pos + (0 if source[axis_pos] > 7 else 1)
                others = [other_axis for other_axis in range(3) if other_axis != axis_pos]
                ghost_table[lattice_dir, cell] = 8 * source[others[0]] + source[others[1]]
            elif len(outside) > 1:
                side_table[lattice_dir, cell] = 6
    return side_table, ghost_table


def build_quadrants():
    quad_cells = np.zeros((4, 64), dtype=np.int32)
    for quad in range(4):
        for fine_i in range(8):
            for fine_k in range(8):
                quad_cells[quad, 8 * fine_i + fine_k] = 8 * (4 * (quad // 2) + fine_i // 2) + 4 * (quad % 2) + fine_k // 2
    return quad_cells


def build_offsets():
    velocity_set = velocity_list()
    return [int(64 * velocity_set[lattice_dir][0] + 8 * velocity_set[lattice_dir][1] + velocity_set[lattice_dir][2]) for lattice_dir in range(19)]


def equilibrium(states):
    velocity_f32 = jnp.asarray(np.array(velocity_list()), dtype=jnp.float32)
    weight_f32 = jnp.asarray(np.array([1.0 / 3.0] + [1.0 / 18.0] * 6 + [1.0 / 36.0] * 12), dtype=jnp.float32)
    density = jnp.sum(states, axis=1)
    momentum = jnp.einsum("qa,mqn->man", velocity_f32, states, precision=lax.Precision.HIGHEST)
    velocity = momentum / density[:, None, :]
    project = jnp.einsum("qa,man->mqn", velocity_f32, velocity, precision=lax.Precision.HIGHEST)
    square = jnp.sum(velocity * velocity, axis=1)
    return weight_f32[None, :, None] * density[:, None, :] * (1.0 + 3.0 * project + 4.5 * project * project - 1.5 * square[:, None, :])


def collide(states):
    relax_matrix = jnp.asarray(build_relax(), dtype=jnp.float32)
    balance = equilibrium(states)
    return states - jnp.einsum("pq,mqn->mpn", relax_matrix, states - balance, precision=lax.Precision.HIGHEST)


def layer_of(relaxed, face_dir):
    crossing_sets = build_crossing()
    layer_cells = build_layers()
    picked = jnp.take(relaxed, jnp.asarray(crossing_sets[face_dir], dtype=jnp.int32), axis=1)
    picked = jnp.take(picked, jnp.asarray(layer_cells[face_dir ^ 1], dtype=jnp.int32), axis=2)
    return picked.reshape(relaxed.shape[0], 320)


def interface_values(coarse_tiles):
    crossing_sets = build_crossing()
    coarse_ratio = 0.6 / 1.1
    total = coarse_tiles.shape[0]
    outputs = []
    for time_frac in (0.0, 0.5):
        blended = (1.0 - time_frac) * coarse_tiles[:, 0] + time_frac * coarse_tiles[:, 1]
        balance = equilibrium(blended)
        ghost_vals = balance + coarse_ratio * (blended - balance)
        chosen = jnp.take(ghost_vals, jnp.asarray(crossing_sets[2], dtype=jnp.int32), axis=1)
        outputs.append(chosen.reshape(total, 320))
    return jnp.stack(outputs, axis=1)


def spread_quadrant(picked, quadrant):
    quad_table = jnp.asarray(build_quadrants(), dtype=jnp.int32)
    total = picked.shape[0]
    ghost_view = picked.reshape(total, 2, 5, 64)
    cell_index = jnp.take(quad_table, quadrant, axis=0)
    cell_index = jnp.broadcast_to(cell_index[:, None, None, :], (total, 2, 5, 64))
    return jnp.take_along_axis(ghost_view, cell_index, axis=3).reshape(total, 2, 320)


def stream(relaxed, initial, ghosts, present, solid):
    crossing_sets = build_crossing()
    source_side, ghost_cell = build_sources()
    shift_offsets = build_offsets()
    opposite_dir = opposite_list()
    total = relaxed.shape[0]
    fluid = solid == 0
    ghost_view = ghosts.reshape(total, 6, 5, 64)
    pulled = []
    for lattice_dir in range(19):
        moved = jnp.roll(relaxed[:, lattice_dir], shift_offsets[lattice_dir], axis=1)
        usable = jnp.roll(fluid, shift_offsets[lattice_dir], axis=1)
        for face_dir in range(6):
            if lattice_dir in crossing_sets[face_dir]:
                slot_pos = crossing_sets[face_dir].index(lattice_dir)
                through = jnp.asarray(source_side[lattice_dir] == face_dir)[None, :]
                fetched = jnp.take(ghost_view[:, face_dir, slot_pos], jnp.asarray(ghost_cell[lattice_dir]), axis=1)
                moved = jnp.where(through, fetched, moved)
                usable = jnp.where(through, present[:, face_dir:face_dir + 1], usable)
        edge_mask = jnp.asarray(source_side[lattice_dir] == 6)[None, :]
        usable = jnp.where(edge_mask, False, usable)
        pulled.append(jnp.where(usable, moved, relaxed[:, opposite_dir[lattice_dir]]))
    read = jnp.stack(pulled, axis=1)
    return jnp.where(fluid[:, None, :], read, initial)


def reference(populations, coarse_faces, neighbors, interface, solid):
    face_ids = jnp.arange(6, dtype=jnp.int32)
    has_coarse = interface[:, 0] >= 0
    present = (neighbors >= 0) | ((face_ids[None, :] == 2) & has_coarse[:, None])
    coarse_vals = interface_values(coarse_faces)
    picked = jnp.take(coarse_vals, jnp.clip(interface[:, 0], 0, CBLOCKS - 1), axis=0)
    fine_ghost = spread_quadrant(picked, interface[:, 1])
    current = populations
    for substep in range(2):
        grouped = current.reshape(N_BLK, BLK_DEV, Q, CELLS)
        relaxed = lax.map(collide, grouped).reshape(BLOCKS, Q, CELLS)
        ghosts = []
        for face_dir in range(6):
            layer = layer_of(relaxed, face_dir)
            fetched = jnp.take(layer, jnp.clip(neighbors[:, face_dir], 0, BLOCKS - 1), axis=0)
            if face_dir == 2:
                fetched = jnp.where(has_coarse[:, None], fine_ghost[:, substep], fetched)
            ghosts.append(fetched)
        current = stream(relaxed, populations, jnp.stack(ghosts, axis=1), present, solid)
    return current
```

```python
import functools

import jax
import jax.numpy as jnp
import numpy as np
from jax import lax
from jax.experimental import pallas as pl
from jax.experimental.pallas import tpu as pltpu
from jax.sharding import PartitionSpec as P

MESH = pl.DeviceIdType.MESH
F32 = jnp.float32
BF16 = jnp.bfloat16
I32 = jnp.int32

VEL = [
    (0, 0, 0),
    (1, 0, 0),
    (-1, 0, 0),
    (0, 1, 0),
    (0, -1, 0),
    (0, 0, 1),
    (0, 0, -1),
    (1, 1, 0),
    (-1, -1, 0),
    (1, -1, 0),
    (-1, 1, 0),
    (1, 0, 1),
    (-1, 0, -1),
    (1, 0, -1),
    (-1, 0, 1),
    (0, 1, 1),
    (0, -1, -1),
    (0, 1, -1),
    (0, -1, 1),
]
OPP = [VEL.index((-x, -y, -z)) for x, y, z in VEL]
CROSS = [
    [q for q in range(19) if VEL[q][d // 2] == (-1 if d % 2 == 0 else 1)] for d in range(6)
]
BIT = [9 * (x + 1) + 3 * (y + 1) + (z + 1) for x, y, z in VEL]
BLK = 32
TILE = 128
ROWS = 8


def relax_delta(f):
    s = 1.0 / 0.6
    sx, dx = f[1] + f[2], f[1] - f[2]
    sy, dy = f[3] + f[4], f[3] - f[4]
    sz, dz = f[5] + f[6], f[5] - f[6]
    s7, d7 = f[7] + f[8], f[7] - f[8]
    s9, d9 = f[9] + f[10], f[9] - f[10]
    s11, d11 = f[11] + f[12], f[11] - f[12]
    s13, d13 = f[13] + f[14], f[13] - f[14]
    s15, d15 = f[15] + f[16], f[15] - f[16]
    s17, d17 = f[17] + f[18], f[17] - f[18]
    sa, ta = s7 + s9, s7 - s9
    sb, tb = s11 + s13, s11 - s13
    sc, tc = s15 + s17, s15 - s17
    ax, ay = d7 + d9, d7 - d9
    bx, bz = d11 + d13, d11 - d13
    cy, cz = d15 + d17, d15 - d17
    x2, mx = ax + bx, ax - bx
    y2, my = ay + cy, cy - ay
    z2, mz = bz + cz, bz - cz
    jx, jy, jz = dx + x2, dy + y2, dz + z2
    ab = sa + sb
    s2 = ab + sc
    yz = sy + sz
    s1 = sx + yz
    rho = f[0] + (s1 + s2)
    inv = 1.0 / rho
    ux, uy, uz = jx * inv, jy * inv, jz * inv
    xx, yy, zz = jx * ux, jy * uy, jz * uz
    jj = (xx + yy) + zz
    m1 = (s2 - f[0]) - jj
    m2 = 9.0 * f[0] - 7.0 * s1 - 2.0 * s2 + 5.5 * jj
    c1 = m1 * (19.0 * 1.19 / 2394.0)
    c2 = m2 * (1.4 / 252.0)
    a9 = (sx + sx) - yz
    b9 = ab - (sc + sc)
    e9 = (xx + xx) - (yy + zz)
    c9 = (a9 + b9 - e9) * (s / 36.0)
    c10 = (b9 - 2.0 * a9 + 0.5 * e9) * (1.4 / 72.0)
    a11 = sy - sz
    b11 = sa - sb
    e11 = yy - zz
    c11 = (a11 + b11 - e11) * (s / 12.0)
    c12 = (b11 - 2.0 * a11 + 0.5 * e11) * (1.4 / 24.0)
    c13 = (ta - jx * uy) * (s / 4.0)
    c14 = (tc - jy * uz) * (s / 4.0)
    c15 = (tb - jx * uz) * (s / 4.0)
    g = (5.0 / 3.0) * 1.2 / 40.0
    c4 = (x2 - 2.0 * dx) * g
    c6 = (y2 - 2.0 * dy) * g
    c8 = (z2 - 2.0 * dz) * g
    h = 1.98 / 8.0
    c16, c17, c18 = mx * h, my * h, mz * h
    r0 = 12.0 * c2 - 30.0 * c1
    ra = -11.0 * c1 - 4.0 * c2
    rd = 8.0 * c1 + c2
    p9 = c9 - 2.0 * c10
    p11 = c11 - 2.0 * c12
    n9 = c9 + c10
    n11 = c11 + c12
    ex = ra + 2.0 * p9
    et = ra - p9
    ey, ez = et + p11, et - p11
    rt = rd + n9
    exy, exz = rt + n11, rt - n11
    eyz = rd - 2.0 * n9
    ox, oy, oz = -4.0 * c4, -4.0 * c6, -4.0 * c8
    xa, ya = c4 + c16, c6 - c17
    xb, zb = c4 - c16, c8 + c18
    yc, zc = c6 + c17, c8 - c18
    e7, e9_ = exy + c13, exy - c13
    e11_, e13 = exz + c15, exz - c15
    e15, e17 = eyz + c14, eyz - c14
    o7, o9 = xa + ya, xa - ya
    o11, o13 = xb + zb, xb - zb
    o15, o17 = yc + zc, yc - zc
    out = [f[0] - r0]
    for q, even, odd in (
        (1, ex, ox),
        (3, ey, oy),
        (5, ez, oz),
        (7, e7, o7),
        (9, e9_, o9),
        (11, e11_, o11),
        (13, e13, o13),
        (15, e15, o15),
        (17, e17, o17),
    ):
        out.append(f[q] - (even + odd))
        out.append(f[q + 1] - (even - odd))
    return out


def split(x):
    hi = x.astype(BF16)
    lo = (x - hi.astype(F32)).astype(BF16)
    return jnp.concatenate([hi, lo], axis=0)


def roll(x, by):
    by %= TILE
    return pltpu.roll(x, by, 1) if by else x


def lanes():
    return lax.broadcasted_iota(I32, (ROWS, TILE), 1)


def face_lanes(d, t, lane):
    if d == 0:
        return lane >= 64 if t == 3 else None
    if d == 1:
        return lane < 64 if t == 0 else None
    pos = ((lane >> 3) & 7) if d < 4 else (lane & 7)
    return pos == (7 if d % 2 == 0 else 0)


def cols(t):
    return pl.ds(t * TILE, TILE)


def rows_of(r):
    return pl.ds(pl.multiple_of(r * ROWS, ROWS), ROWS)


def store_post(post, ref, packs, xs, rows, t, lane):
    for q in range(19):
        ref[q, rows, cols(t)] = post[q]
    high = lane & 7
    mid = (lane >> 3) & 7
    for d in range(2, 6):
        acc = post[CROSS[d][0]]
        for s in range(1, 5):
            step = (8 if d < 4 else 1) * s
            pos = mid if d < 4 else high
            by, at = (step, s) if d % 2 == 0 else (-step, 7 - s)
            acc = jnp.where(pos == at, roll(post[CROSS[d][s]], by), acc)
        packs[d - 2, rows, cols(t)] = acc
    if t in (0, 3):
        d = 0 if t == 0 else 1
        keep = lane < 64 if t == 0 else lane >= 64
        for s in range(2):
            a, b = CROSS[d][2 * s], CROSS[d][2 * s + 1]
            xs[d, rows, cols(s)] = jnp.where(keep, post[a], roll(post[b], 64))
        xs[d, rows, cols(2)] = post[CROSS[d][4]]


def stream(ref, gh, gx, code_ref, rows, t, lane):
    post = [ref[q, rows, cols(t)] for q in range(19)]
    code = code_ref[rows, cols(t)]
    upper = lane >= 64

    def merged(ex, here, load, edge):
        if ex == 0:
            return here
        near = t - ex
        if 0 <= near <= 3:
            other = load(near)
        else:
            other = edge
        if other is None:
            return here
        return jnp.where(upper, other, here) if ex == 1 else jnp.where(upper, here, other)

    out = [post[0]]
    for q in range(1, 19):
        ex, ey, ez = VEL[q]
        edge = None
        if ex != 0 and not 0 <= t - ex <= 3:
            d = 0 if ex == -1 else 1
            n = CROSS[d].index(q)
            edge = gx[d, rows, cols(n // 2)]
            if n % 2:
                edge = roll(edge, 64)
        base = 64 * ex
        src = merged(ex, post[q], lambda u: ref[q, rows, cols(u)], edge)
        moved = roll(src, base + 8 * ey + ez)
        for d, comp in ((2 if ey < 0 else 3, ey), (4 if ez < 0 else 5, ez)):
            if comp == 0:
                continue
            s = CROSS[d].index(q)
            if d < 4:
                off = (56 - 8 * s) * (1 if d == 2 else -1) + base + ez
            else:
                off = (7 - s) * (1 if d == 4 else -1) + base + 8 * ey
            g = merged(
                ex, gh[d - 2, rows, cols(t)], lambda u: gh[d - 2, rows, cols(u)], None
            )
            moved = jnp.where(face_lanes(d, t, lane), roll(g, off), moved)
        usable = (code & (1 << BIT[q])) != 0
        out.append(jnp.where(usable, moved, post[OPP[q]]))
    return out


def kernel(
    n,
    pops,
    coarse,
    nbr,
    itf,
    solid,
    out,
    f,
    pa,
    pb,
    ov,
    packs,
    gh,
    gxl,
    gx,
    xs,
    xr,
    cfv,
    nv,
    iv,
    sv,
    cs,
    cr,
    gc,
    code,
    pw,
    pyz,
    pxl,
    pxr,
    pc,
    in_sem,
    out_sem,
    send_sem,
    recv_sem,
):
    me = lax.axis_index("blk")
    nxt = lax.rem(me + 1, n)
    prv = lax.rem(me + n - 1, n)

    barrier = pltpu.get_barrier_semaphore()
    for peer in (prv, nxt):
        pl.semaphore_signal(barrier, inc=1, device_id=(peer,), device_id_type=MESH)

    def fetch(k, src, dst):
        c = pltpu.make_async_copy(src, dst, in_sem.at[k])
        c.start()
        return c

    def tile_of(ref, t, w=1):
        return ref.at[:, :, pl.ds(t * TILE, w * TILE)]

    in3 = fetch(0, tile_of(pops, 3), tile_of(f, 3))
    in0 = fetch(1, tile_of(pops, 0), tile_of(f, 0))
    inc = fetch(2, coarse, cfv)
    inn = fetch(3, nbr, nv)
    ini = fetch(4, itf, iv)
    ins = fetch(5, solid, sv)
    in12 = fetch(6, tile_of(pops, 1, 2), tile_of(f, 1, 2))

    def send(k, src, dst, peer):
        c = pltpu.make_async_remote_copy(
            src_ref=src,
            dst_ref=dst,
            send_sem=send_sem.at[k],
            recv_sem=recv_sem.at[k],
            device_id=(peer,),
            device_id_type=MESH,
        )
        c.start()
        return c

    lane = lanes()

    def first_collide(t):
        def step(r, carry):
            rows = rows_of(r)
            post = relax_delta([f[q, rows, cols(t)] for q in range(19)])
            store_post(post, pa, packs, xs.at[0], rows, t, lane)
            return carry

        lax.fori_loop(0, BLK // ROWS, step, 0)

    in3.wait()
    first_collide(3)
    pl.semaphore_wait(barrier, 2)
    sends = [send(1, xs.at[0, 1], xr.at[0, 1], nxt)]
    in0.wait()
    first_collide(0)
    sends.append(send(0, xs.at[0, 0], xr.at[0, 0], prv))

    inc.wait()
    ratio = 0.6 / 1.1
    cs[...] = jnp.zeros((2, 16, TILE), F32)
    for c in range(2):
        row = lax.broadcasted_iota(I32, (2, 64), 0)
        w0 = jnp.where(row == 0, 0.0, 0.5)
        w1 = jnp.where(row == 0, 1.0, 0.5)
        hs = []
        for q in range(19):
            both = cfv[c, q, :, :]
            hs.append(w1 * both + w0 * both[0:1, :])
        rho = functools.reduce(lambda a, b: a + b, hs)
        mom = []
        for axis in range(3):
            plus = functools.reduce(
                lambda a, b: a + b, [hs[q] for q in range(19) if VEL[q][axis] == 1]
            )
            minus = functools.reduce(
                lambda a, b: a + b, [hs[q] for q in range(19) if VEL[q][axis] == -1]
            )
            mom.append(plus - minus)
        inv = 1.0 / rho
        vel = [m * inv for m in mom]
        sq = 1.0 - 1.5 * (vel[0] * vel[0] + vel[1] * vel[1] + vel[2] * vel[2])
        for s, q in enumerate(CROSS[2]):
            proj = None
            for axis in range(3):
                if VEL[q][axis]:
                    term = vel[axis] if VEL[q][axis] == 1 else -vel[axis]
                    proj = term if proj is None else proj + term
            weight = 1.0 / 18.0 if q < 7 else 1.0 / 36.0
            eq = (weight * rho) * (sq + 3.0 * proj + 4.5 * proj * proj)
            val = eq + ratio * (hs[q] - eq)
            for k in range(2):
                cs[k, pl.ds(8 * c + s, 1), 0:64] = val[k : k + 1, :]
    sends.append(send(4, cs, cr, prv))

    in12.wait()
    first_collide(1)
    first_collide(2)

    inn.wait()
    ini.wait()
    eye = lax.broadcasted_iota(I32, (BLK, BLK), 0) == lax.broadcasted_iota(I32, (BLK, BLK), 1)

    def column(row):
        wide = jnp.broadcast_to(row.astype(F32), (BLK, BLK))
        return jnp.sum(jnp.where(eye, wide, 0.0), axis=1, keepdims=True)

    face = [column(nv[d : d + 1, :]) for d in range(6)]
    cb = column(iv[0:1, :])
    quad = column(iv[1:2, :])
    first = (me * BLK).astype(F32)
    slot = (lax.broadcasted_iota(I32, (BLK, 2 * BLK), 1) & (BLK - 1)).astype(F32)
    local = [jnp.where(v >= 0.0, v - first, -1.0) for v in face]
    one = [jnp.where(v == slot, 1.0, 0.0).astype(BF16) for v in local]
    for d in range(2):
        pxl[d] = one[d]
    for d in range(4):
        pyz[d] = one[d + 2]
    for d, shift in ((0, -float(BLK)), (1, float(BLK))):
        far = jnp.where(face[d] >= 0.0, face[d] - first + shift, -1.0)
        pxr[d] = jnp.where(far == slot, 1.0, 0.0).astype(BF16)
    key = jnp.where(cb >= 0.0, 2.0 * quad + cb - 2.0 * (me + 1).astype(F32), -1.0)
    group = ((lax.broadcasted_iota(I32, (BLK, TILE), 1) & 63) >> 3).astype(F32)
    pc[...] = jnp.where(key == group, 1.0, 0.0).astype(BF16)
    for d in range(6):
        there = face[d] >= 0.0
        if d == 2:
            there = there | (cb >= 0.0)
        bits = sum(1 << BIT[q] for q in CROSS[d])
        pw[d] = jnp.broadcast_to(jnp.where(there, -1, ~bits), (BLK, TILE))

    ins.wait()
    static = []
    for t in range(4):
        word = jnp.full((ROWS, TILE), -1, I32)
        for q in range(7, 19):
            axes = [a for a in range(3) if VEL[q][a]]
            masks = [face_lanes(2 * a + (0 if VEL[q][a] < 0 else 1), t, lane) for a in axes]
            if all(m is not None for m in masks):
                word = jnp.where(masks[0] & masks[1], word & ~(1 << BIT[q]), word)
        static.append(word)

    def code_step(r, carry):
        rows = rows_of(r)
        yz = []
        for t in range(4):
            fl = 1 - sv[rows, cols(t)]
            wz = roll(fl, -1) | (fl << 1) | (roll(fl, 1) << 2)
            yz.append(roll(wz, -8) | (wz << 3) | (roll(wz, 8) << 6))
        ones = jnp.full((ROWS, TILE), -1, I32)
        for t in range(4):
            below = yz[t - 1] if t > 0 else ones
            above = yz[t + 1] if t < 3 else ones
            up = roll(jnp.where(lane >= 64, below, yz[t]), 64) << 18
            down = roll(jnp.where(lane < 64, above, yz[t]), 64) & 511
            word = (up | (yz[t] << 9) | down) & static[t]
            for d in range(6):
                m = face_lanes(d, t, lane)
                if m is not None:
                    word = word & jnp.where(m, pw[d, rows, :], -1)
            code[rows, cols(t)] = word
        return carry

    lax.fori_loop(0, BLK // ROWS, code_step, 0)

    sends[2].wait_recv()
    kk = (lane & 7) >> 1
    at = (lane >> 3) & 7
    srow = lax.broadcasted_iota(I32, (ROWS, TILE), 0)
    for k in range(2):
        parts = []
        for quadrant in range(4):
            for c in range(2):
                vals = cr[k, 8 * c : 8 * c + 8, :]
                spread = []
                for t in range(4):
                    idx = kk + (32 * (quadrant // 2) + 4 * (quadrant % 2) + 8 * t)
                    got = jnp.take_along_axis(vals, idx, axis=1, mode="promise_in_bounds")
                    spread.append(jnp.where(at == srow, got, 0.0))
                parts.append(jnp.concatenate(spread, axis=1))
        table = jnp.concatenate(parts, axis=0)
        gc[k] = jnp.dot(pc[...], split(table), preferred_element_type=F32)

    def gather_local(sub):
        for d in range(4):
            g = jnp.dot(pyz[d], split(packs[d]), preferred_element_type=F32)
            if d == 0:
                g = g + gc[sub]
            gh[d] = g
        for d in range(2):
            gxl[d] = jnp.dot(pxl[d], split(xs[sub, d]), preferred_element_type=F32)

    def gather_remote(sub, pair):
        for d in (1, 0):
            pair[d].wait_recv()
            far = jnp.dot(pxr[d], split(xr[sub, d]), preferred_element_type=F32)
            gx[d] = gxl[d] + far

    def second_collide(t):
        def step(r, carry):
            rows = rows_of(r)
            cur = stream(pa, gh, gx, code, rows, t, lane)
            store_post(relax_delta(cur), pb, packs, xs.at[1], rows, t, lane)
            return carry

        lax.fori_loop(0, BLK // ROWS, step, 0)

    def finish(t):
        def step(r, carry):
            rows = rows_of(r)
            cur = stream(pb, gh, gx, code, rows, t, lane)
            wet = (code[rows, cols(t)] & (1 << BIT[0])) != 0
            for q in range(19):
                ov[q, rows, cols(t)] = jnp.where(wet, cur[q], f[q, rows, cols(t)])
            return carry

        lax.fori_loop(0, BLK // ROWS, step, 0)

    gather_local(0)
    second_collide(1)
    second_collide(2)
    gather_remote(0, (sends[1], sends[0]))
    second_collide(3)
    sends.append(send(3, xs.at[1, 1], xr.at[1, 1], nxt))
    second_collide(0)
    sends.append(send(2, xs.at[1, 0], xr.at[1, 0], prv))

    gather_local(1)
    outs = []

    def emit(k, t, w):
        c = pltpu.make_async_copy(tile_of(ov, t, w), tile_of(out, t, w), out_sem.at[k])
        c.start()
        outs.append(c)

    finish(1)
    finish(2)
    emit(0, 1, 2)
    gather_remote(1, (sends[4], sends[3]))
    finish(3)
    emit(1, 3, 1)
    finish(0)
    emit(2, 0, 1)
    for c in sends:
        c.wait_send()
    for c in outs:
        c.wait()


def body(populations, coarse_faces, neighbors, interface, solid):
    n = lax.axis_size("blk")
    pops = jnp.transpose(populations, (1, 0, 2))
    coarse = jnp.transpose(coarse_faces, (0, 2, 1, 3))
    anywhere = pl.BlockSpec(memory_space=pl.ANY)
    vm = pltpu.VMEM
    big = vm((19, BLK, 512), F32)
    done = pl.pallas_call(
        functools.partial(kernel, n),
        out_shape=jax.ShapeDtypeStruct((19, BLK, 512), F32),
        in_specs=[anywhere] * 5,
        out_specs=anywhere,
        scratch_shapes=[
            big,
            big,
            big,
            big,
            vm((4, BLK, 512), F32),
            vm((4, BLK, 512), F32),
            vm((2, BLK, 384), F32),
            vm((2, BLK, 384), F32),
            vm((2, 2, BLK, 384), F32),
            vm((2, 2, BLK, 384), F32),
            vm((2, 19, 2, 64), F32),
            vm((6, BLK), I32),
            vm((2, BLK), I32),
            vm((BLK, 512), I32),
            vm((2, 16, TILE), F32),
            vm((2, 16, TILE), F32),
            vm((2, BLK, 512), F32),
            vm((BLK, 512), I32),
            vm((6, BLK, TILE), I32),
            vm((4, BLK, 2 * BLK), BF16),
            vm((2, BLK, 2 * BLK), BF16),
            vm((2, BLK, 2 * BLK), BF16),
            vm((BLK, TILE), BF16),
            pltpu.SemaphoreType.DMA((7,)),
            pltpu.SemaphoreType.DMA((3,)),
            pltpu.SemaphoreType.DMA((5,)),
            pltpu.SemaphoreType.DMA((5,)),
        ],
        compiler_params=pltpu.CompilerParams(
            collective_id=0, has_side_effects=True, vmem_limit_bytes=40 * 2**20
        ),
    )(pops, coarse, neighbors.T, interface.T, solid)
    return jnp.transpose(done, (1, 0, 2))


def solution(mesh):
    placed = (
        P("blk", None, None),
        P("blk", None, None, None),
        P("blk", None),
        P("blk", None),
        P("blk", None),
    )
    return jax.shard_map(
        body, mesh=mesh, in_specs=placed, out_specs=P("blk", None, None), check_vma=False
    )
```

```python
import functools

import jax
import jax.numpy as jnp
import numpy as np
from jax import lax
from jax.experimental import pallas as pl
from jax.experimental.pallas import tpu as pltpu
from jax.sharding import PartitionSpec as P

MESH = pl.DeviceIdType.MESH
F32 = jnp.float32
BF16 = jnp.bfloat16
I32 = jnp.int32

VEL = [
    (0, 0, 0),
    (1, 0, 0),
    (-1, 0, 0),
    (0, 1, 0),
    (0, -1, 0),
    (0, 0, 1),
    (0, 0, -1),
    (1, 1, 0),
    (-1, -1, 0),
    (1, -1, 0),
    (-1, 1, 0),
    (1, 0, 1),
    (-1, 0, -1),
    (1, 0, -1),
    (-1, 0, 1),
    (0, 1, 1),
    (0, -1, -1),
    (0, 1, -1),
    (0, -1, 1),
]
OPP = [VEL.index((-x, -y, -z)) for x, y, z in VEL]
CROSS = [
    [q for q in range(19) if VEL[q][d // 2] == (-1 if d % 2 == 0 else 1)] for d in range(6)
]
BIT = [9 * (x + 1) + 3 * (y + 1) + (z + 1) for x, y, z in VEL]
BLK = 32
TILE = 128


def relax_delta(f):
    s = 1.0 / 0.6
    sx, dx = f[1] + f[2], f[1] - f[2]
    sy, dy = f[3] + f[4], f[3] - f[4]
    sz, dz = f[5] + f[6], f[5] - f[6]
    s7, d7 = f[7] + f[8], f[7] - f[8]
    s9, d9 = f[9] + f[10], f[9] - f[10]
    s11, d11 = f[11] + f[12], f[11] - f[12]
    s13, d13 = f[13] + f[14], f[13] - f[14]
    s15, d15 = f[15] + f[16], f[15] - f[16]
    s17, d17 = f[17] + f[18], f[17] - f[18]
    sa, ta = s7 + s9, s7 - s9
    sb, tb = s11 + s13, s11 - s13
    sc, tc = s15 + s17, s15 - s17
    ax, ay = d7 + d9, d7 - d9
    bx, bz = d11 + d13, d11 - d13
    cy, cz = d15 + d17, d15 - d17
    x2, mx = ax + bx, ax - bx
    y2, my = ay + cy, cy - ay
    z2, mz = bz + cz, bz - cz
    jx, jy, jz = dx + x2, dy + y2, dz + z2
    ab = sa + sb
    s2 = ab + sc
    yz = sy + sz
    s1 = sx + yz
    rho = f[0] + (s1 + s2)
    inv = 1.0 / rho
    ux, uy, uz = jx * inv, jy * inv, jz * inv
    xx, yy, zz = jx * ux, jy * uy, jz * uz
    jj = (xx + yy) + zz
    m1 = (s2 - f[0]) - jj
    m2 = 9.0 * f[0] - 7.0 * s1 - 2.0 * s2 + 5.5 * jj
    c1 = m1 * (19.0 * 1.19 / 2394.0)
    c2 = m2 * (1.4 / 252.0)
    a9 = (sx + sx) - yz
    b9 = ab - (sc + sc)
    e9 = (xx + xx) - (yy + zz)
    c9 = (a9 + b9 - e9) * (s / 36.0)
    c10 = (b9 - 2.0 * a9 + 0.5 * e9) * (1.4 / 72.0)
    a11 = sy - sz
    b11 = sa - sb
    e11 = yy - zz
    c11 = (a11 + b11 - e11) * (s / 12.0)
    c12 = (b11 - 2.0 * a11 + 0.5 * e11) * (1.4 / 24.0)
    c13 = (ta - jx * uy) * (s / 4.0)
    c14 = (tc - jy * uz) * (s / 4.0)
    c15 = (tb - jx * uz) * (s / 4.0)
    g = (5.0 / 3.0) * 1.2 / 40.0
    c4 = (x2 - 2.0 * dx) * g
    c6 = (y2 - 2.0 * dy) * g
    c8 = (z2 - 2.0 * dz) * g
    h = 1.98 / 8.0
    c16, c17, c18 = mx * h, my * h, mz * h
    r0 = 12.0 * c2 - 30.0 * c1
    ra = -11.0 * c1 - 4.0 * c2
    rd = 8.0 * c1 + c2
    p9 = c9 - 2.0 * c10
    p11 = c11 - 2.0 * c12
    n9 = c9 + c10
    n11 = c11 + c12
    ex = ra + 2.0 * p9
    et = ra - p9
    ey, ez = et + p11, et - p11
    rt = rd + n9
    exy, exz = rt + n11, rt - n11
    eyz = rd - 2.0 * n9
    ox, oy, oz = -4.0 * c4, -4.0 * c6, -4.0 * c8
    xa, ya = c4 + c16, c6 - c17
    xb, zb = c4 - c16, c8 + c18
    yc, zc = c6 + c17, c8 - c18
    e7, e9_ = exy + c13, exy - c13
    e11_, e13 = exz + c15, exz - c15
    e15, e17 = eyz + c14, eyz - c14
    o7, o9 = xa + ya, xa - ya
    o11, o13 = xb + zb, xb - zb
    o15, o17 = yc + zc, yc - zc
    out = [f[0] - r0]
    for q, even, odd in (
        (1, ex, ox),
        (3, ey, oy),
        (5, ez, oz),
        (7, e7, o7),
        (9, e9_, o9),
        (11, e11_, o11),
        (13, e13, o13),
        (15, e15, o15),
        (17, e17, o17),
    ):
        out.append(f[q] - (even + odd))
        out.append(f[q + 1] - (even - odd))
    return out


def split(x):
    hi = x.astype(BF16)
    lo = (x - hi.astype(F32)).astype(BF16)
    return jnp.concatenate([hi, lo], axis=0)


def roll(x, by):
    by %= TILE
    return pltpu.roll(x, by, 1) if by else x


def lanes():
    return lax.broadcasted_iota(I32, (BLK, TILE), 1)


def face_lanes(d, t, lane):
    if d == 0:
        return lane >= 64 if t == 3 else None
    if d == 1:
        return lane < 64 if t == 0 else None
    pos = ((lane >> 3) & 7) if d < 4 else (lane & 7)
    return pos == (7 if d % 2 == 0 else 0)


def cols(t):
    return pl.ds(t * TILE, TILE)


def store_post(post, ref, packs, xs, t, lane):
    for q in range(19):
        ref[q, :, cols(t)] = post[q]
    high = lane & 7
    mid = (lane >> 3) & 7
    for d in range(2, 6):
        acc = post[CROSS[d][0]]
        for s in range(1, 5):
            step = (8 if d < 4 else 1) * s
            pos = mid if d < 4 else high
            by, at = (step, s) if d % 2 == 0 else (-step, 7 - s)
            acc = jnp.where(pos == at, roll(post[CROSS[d][s]], by), acc)
        packs[d - 2, :, cols(t)] = acc
    if t in (0, 3):
        d = 0 if t == 0 else 1
        keep = lane < 64 if t == 0 else lane >= 64
        for s in range(2):
            a, b = CROSS[d][2 * s], CROSS[d][2 * s + 1]
            xs[d, :, cols(s)] = jnp.where(keep, post[a], roll(post[b], 64))
        xs[d, :, cols(2)] = post[CROSS[d][4]]


def stream(ref, gh, gx, code_ref, t, lane):
    post = [ref[q, :, cols(t)] for q in range(19)]
    code = code_ref[:, cols(t)]
    upper = lane >= 64

    def merged(ex, here, load, edge):
        if ex == 0:
            return here
        near = t - ex
        if 0 <= near <= 3:
            other = load(near)
        else:
            other = edge
        if other is None:
            return here
        return jnp.where(upper, other, here) if ex == 1 else jnp.where(upper, here, other)

    out = [post[0]]
    for q in range(1, 19):
        ex, ey, ez = VEL[q]
        edge = None
        if ex != 0 and not 0 <= t - ex <= 3:
            d = 0 if ex == -1 else 1
            n = CROSS[d].index(q)
            edge = gx[d, :, cols(n // 2)]
            if n % 2:
                edge = roll(edge, 64)
        base = 64 * ex
        src = merged(ex, post[q], lambda u: ref[q, :, cols(u)], edge)
        moved = roll(src, base + 8 * ey + ez)
        for d, comp in ((2 if ey < 0 else 3, ey), (4 if ez < 0 else 5, ez)):
            if comp == 0:
                continue
            s = CROSS[d].index(q)
            if d < 4:
                off = (56 - 8 * s) * (1 if d == 2 else -1) + base + ez
            else:
                off = (7 - s) * (1 if d == 4 else -1) + base + 8 * ey
            g = merged(
                ex, gh[d - 2, :, cols(t)], lambda u: gh[d - 2, :, cols(u)], None
            )
            moved = jnp.where(face_lanes(d, t, lane), roll(g, off), moved)
        usable = (code & (1 << BIT[q])) != 0
        out.append(jnp.where(usable, moved, post[OPP[q]]))
    return out


def coarse_ghost(cfv, cs):
    ratio = 0.6 / 1.1
    cs[...] = jnp.zeros((2, 16, TILE), F32)
    row = lax.broadcasted_iota(I32, (2, 64), 0)
    w0 = jnp.where(row == 0, 0.0, 0.5)
    w1 = jnp.where(row == 0, 1.0, 0.5)

    def total(items):
        return functools.reduce(lambda a, b: a + b, items)

    for c in range(2):
        hs = []
        for q in range(19):
            both = cfv[c, q, :, :]
            hs.append(w1 * both + w0 * both[0:1, :])
        rho = total(hs)
        inv = 1.0 / rho
        vel = []
        for axis in range(3):
            plus = total([hs[q] for q in range(19) if VEL[q][axis] == 1])
            minus = total([hs[q] for q in range(19) if VEL[q][axis] == -1])
            vel.append((plus - minus) * inv)
        sq = 1.0 - 1.5 * (vel[0] * vel[0] + vel[1] * vel[1] + vel[2] * vel[2])
        for s, q in enumerate(CROSS[2]):
            proj = total(
                [v if e == 1 else -v for v, e in zip(vel, VEL[q]) if e]
            )
            weight = 1.0 / 18.0 if q < 7 else 1.0 / 36.0
            eq = (weight * rho) * (sq + 3.0 * proj + 4.5 * proj * proj)
            val = eq + ratio * (hs[q] - eq)
            for k in range(2):
                cs[k, pl.ds(8 * c + s, 1), 0:64] = val[k : k + 1, :]


def build_tables(me, nv, iv, pyz, pxl, pxr, pc, pw):
    row, col = (lax.broadcasted_iota(I32, (BLK, BLK), a) for a in (0, 1))
    eye = row == col

    def column(vals):
        wide = jnp.broadcast_to(vals.astype(F32), (BLK, BLK))
        return jnp.sum(jnp.where(eye, wide, 0.0), axis=1, keepdims=True)

    face = [column(nv[d : d + 1, :]) for d in range(6)]
    cb = column(iv[0:1, :])
    quad = column(iv[1:2, :])
    first = (me * BLK).astype(F32)
    slot = (lax.broadcasted_iota(I32, (BLK, 2 * BLK), 1) & (BLK - 1)).astype(F32)
    for d in range(6):
        local = jnp.where(face[d] >= 0.0, face[d] - first, -1.0)
        one = jnp.where(local == slot, 1.0, 0.0).astype(BF16)
        if d < 2:
            pxl[d] = one
            shift = -float(BLK) if d == 0 else float(BLK)
            there = jnp.where(face[d] >= 0.0, face[d] - first + shift, -1.0)
            pxr[d] = jnp.where(there == slot, 1.0, 0.0).astype(BF16)
        else:
            pyz[d - 2] = one
    key = jnp.where(cb >= 0.0, 2.0 * quad + cb - 2.0 * (me + 1).astype(F32), -1.0)
    group = ((lax.broadcasted_iota(I32, (BLK, TILE), 1) & 63) >> 3).astype(F32)
    pc[...] = jnp.where(key == group, 1.0, 0.0).astype(BF16)
    for d in range(6):
        there = face[d] >= 0.0
        if d == 2:
            there = there | (cb >= 0.0)
        bits = sum(1 << BIT[q] for q in CROSS[d])
        pw[d] = jnp.broadcast_to(jnp.where(there, -1, ~bits), (BLK, TILE))


def build_code(sv, pw, code, lane):
    yz = []
    for t in range(4):
        fl = 1 - sv[:, cols(t)]
        wz = roll(fl, -1) | (fl << 1) | (roll(fl, 1) << 2)
        yz.append(roll(wz, -8) | (wz << 3) | (roll(wz, 8) << 6))
    ones = jnp.full((BLK, TILE), -1, I32)
    row = lax.broadcasted_iota(I32, (8, TILE), 1)
    for t in range(4):
        static = jnp.full((8, TILE), -1, I32)
        for q in range(7, 19):
            axes = [a for a in range(3) if VEL[q][a]]
            masks = [face_lanes(2 * a + (0 if VEL[q][a] < 0 else 1), t, row) for a in axes]
            if all(m is not None for m in masks):
                static = jnp.where(masks[0] & masks[1], static & ~(1 << BIT[q]), static)
        static = jnp.concatenate([static] * (BLK // 8), axis=0)
        below = yz[t - 1] if t > 0 else ones
        above = yz[t + 1] if t < 3 else ones
        up = roll(jnp.where(lane >= 64, below, yz[t]), 64) << 18
        down = roll(jnp.where(lane < 64, above, yz[t]), 64) & 511
        word = (up | (yz[t] << 9) | down) & static
        for d in range(6):
            m = face_lanes(d, t, lane)
            if m is not None:
                word = word & jnp.where(m, pw[d], -1)
        code[:, cols(t)] = word


def spread_coarse(cr, pc, gc):
    lane = lax.broadcasted_iota(I32, (8, TILE), 1)
    srow = lax.broadcasted_iota(I32, (8, TILE), 0)
    half = (lane & 7) >> 1
    at = (lane >> 3) & 7
    for k in range(2):
        parts = []
        for quadrant in range(4):
            for c in range(2):
                vals = cr[k, 8 * c : 8 * c + 8, :]
                wide = []
                for t in range(4):
                    idx = half + (32 * (quadrant // 2) + 4 * (quadrant % 2) + 8 * t)
                    got = jnp.take_along_axis(vals, idx, axis=1, mode="promise_in_bounds")
                    wide.append(jnp.where(at == srow, got, 0.0))
                parts.append(jnp.concatenate(wide, axis=1))
        table = jnp.concatenate(parts, axis=0)
        gc[k] = jnp.dot(pc[...], split(table), preferred_element_type=F32)


def kernel(
    n,
    pops,
    coarse,
    nbr,
    itf,
    solid,
    out,
    f,
    pa,
    pb,
    packs,
    gh,
    gxl,
    gx,
    xs,
    xr,
    cfv,
    nv,
    iv,
    sv,
    cs,
    cr,
    gc,
    code,
    pw,
    pyz,
    pxl,
    pxr,
    pc,
    in_sem,
    send_sem,
    recv_sem,
):
    me = lax.axis_index("blk")
    nxt = lax.rem(me + 1, n)
    prv = lax.rem(me + n - 1, n)
    lane = lanes()

    def remote(k, src, dst, peer):
        return pltpu.make_async_remote_copy(
            src_ref=src,
            dst_ref=dst,
            send_sem=send_sem.at[k],
            recv_sem=recv_sem.at[k],
            device_id=(peer,),
            device_id_type=MESH,
        )

    def x_copy(sub, k):
        return remote(2 * sub + k, xs.at[sub, k], xr.at[sub, k], nxt if k else prv)

    def c_copy():
        return remote(4, cs, cr, prv)

    def run(even):
        near, far = (0, 1) if even else (1, 0)
        near_tile, far_tile = (3, 0) if even else (0, 3)
        peers = {0: nxt, 1: prv}
        has_far = me > 0 if even else me < n - 1

        barrier = pltpu.get_barrier_semaphore()

        def greet(peer):
            pl.semaphore_signal(barrier, inc=1, device_id=(peer,), device_id_type=MESH)

        greet(peers[near])
        pl.when(has_far)(lambda: greet(peers[far]))

        def fetch(k, src, dst):
            c = pltpu.make_async_copy(src, dst, in_sem.at[k])
            c.start()
            return c

        def fetch_tiles(k, t, w=1):
            part = pl.ds(t * TILE, w * TILE)
            return fetch(k, pops.at[:, :, part], f.at[:, :, part])

        in_c = fetch(0, coarse, cfv)
        in_far = fetch_tiles(1, far_tile)
        in_near = fetch_tiles(2, near_tile)
        in_n = fetch(3, nbr, nv)
        in_i = fetch(4, itf, iv)
        in_mid = fetch_tiles(5, 1, 2)
        in_s = fetch(6, solid, sv)

        def first_collide(t):
            post = relax_delta([f[q, :, cols(t)] for q in range(19)])
            store_post(post, pa, packs, xs.at[0], t, lane)

        def second_collide(t):
            cur = stream(pa, gh, gx, code, t, lane)
            store_post(relax_delta(cur), pb, packs, xs.at[1], t, lane)

        def finish(t):
            cur = stream(pb, gh, gx, code, t, lane)
            wet = (code[:, cols(t)] & (1 << BIT[0])) != 0
            for q in range(19):
                out[q, :, cols(t)] = jnp.where(wet, cur[q], f[q, :, cols(t)])

        def gather_local(sub):
            for d in range(4):
                g = jnp.dot(pyz[d], split(packs[d]), preferred_element_type=F32)
                gh[d] = g + gc[sub] if d == 0 else g
            for d in range(2):
                gxl[d] = jnp.dot(pxl[d], split(xs[sub, d]), preferred_element_type=F32)

        def take(sub, d):
            x_copy(sub, d).wait_recv()
            got = jnp.dot(pxr[d], split(xr[sub, d]), preferred_element_type=F32)
            gx[d] = gxl[d] + got

        def take_far(sub):
            pl.when(has_far)(lambda: take(sub, far))

            @pl.when(jnp.logical_not(has_far))
            def _():
                gx[far] = gxl[far]

        def send_near(sub):
            x_copy(sub, 1 - near).start()

        def send_far(sub):
            pl.when(has_far)(lambda: x_copy(sub, 1 - far).start())

        in_c.wait()
        coarse_ghost(cfv, cs)
        in_far.wait()
        first_collide(far_tile)
        pl.semaphore_wait(barrier, 1 + has_far.astype(I32))
        if even:
            pl.when(has_far)(lambda: c_copy().start())
        else:
            c_copy().start()
        send_far(0)
        in_near.wait()
        first_collide(near_tile)
        send_near(0)

        in_n.wait()
        in_i.wait()
        build_tables(me, nv, iv, pyz, pxl, pxr, pc, pw)
        in_mid.wait()
        first_collide(1)
        first_collide(2)
        in_s.wait()
        build_code(sv, pw, code, lane)

        if even:
            c_copy().wait_recv()
        else:
            pl.when(has_far)(lambda: c_copy().wait_recv())

            @pl.when(jnp.logical_not(has_far))
            def _():
                cr[...] = jnp.zeros((2, 16, TILE), F32)

        spread_coarse(cr, pc, gc)
        gather_local(0)
        if not even:
            second_collide(1)
            second_collide(2)
        take(0, near)
        second_collide(near_tile)
        send_near(1)
        if even:
            second_collide(1)
            second_collide(2)
        take_far(0)
        second_collide(far_tile)
        send_far(1)

        gather_local(1)
        finish(1)
        finish(2)
        take(1, near)
        finish(near_tile)
        take_far(1)
        finish(far_tile)

        for sub in range(2):
            x_copy(sub, 1 - near).wait_send()
        if not even:
            c_copy().wait_send()

        @pl.when(has_far)
        def _():
            for sub in range(2):
                x_copy(sub, 1 - far).wait_send()
            if even:
                c_copy().wait_send()

    is_even = lax.rem(me, 2) == 0
    pl.when(is_even)(lambda: run(True))
    pl.when(jnp.logical_not(is_even))(lambda: run(False))


def body(populations, coarse_faces, neighbors, interface, solid):
    n = lax.axis_size("blk")
    pops = jnp.transpose(populations, (1, 0, 2))
    coarse = jnp.transpose(coarse_faces, (0, 2, 1, 3))
    ins = (pops, coarse, neighbors.T, interface.T, solid)
    ins = [pltpu.with_memory_space_constraint(v, pltpu.HBM) for v in ins]
    anywhere = pl.BlockSpec(memory_space=pl.ANY)
    vm = pltpu.VMEM
    big = vm((19, BLK, 512), F32)
    done = pl.pallas_call(
        functools.partial(kernel, n),
        out_shape=jax.ShapeDtypeStruct((19, BLK, 512), F32),
        in_specs=[anywhere] * 5,
        out_specs=pl.BlockSpec(memory_space=pltpu.VMEM),
        scratch_shapes=[
            big,
            big,
            big,
            vm((4, BLK, 512), F32),
            vm((4, BLK, 512), F32),
            vm((2, BLK, 384), F32),
            vm((2, BLK, 384), F32),
            vm((2, 2, BLK, 384), F32),
            vm((2, 2, BLK, 384), F32),
            vm((2, 19, 2, 64), F32),
            vm((6, BLK), I32),
            vm((2, BLK), I32),
            vm((BLK, 512), I32),
            vm((2, 16, TILE), F32),
            vm((2, 16, TILE), F32),
            vm((2, BLK, 512), F32),
            vm((BLK, 512), I32),
            vm((6, BLK, TILE), I32),
            vm((4, BLK, 2 * BLK), BF16),
            vm((2, BLK, 2 * BLK), BF16),
            vm((2, BLK, 2 * BLK), BF16),
            vm((BLK, TILE), BF16),
            pltpu.SemaphoreType.DMA((7,)),
            pltpu.SemaphoreType.DMA((5,)),
            pltpu.SemaphoreType.DMA((5,)),
        ],
        compiler_params=pltpu.CompilerParams(
            collective_id=0, has_side_effects=True, vmem_limit_bytes=40 * 2**20
        ),
    )(*ins)
    return jnp.transpose(done, (1, 0, 2))


def solution(mesh):
    placed = (
        P("blk", None, None),
        P("blk", None, None, None),
        P("blk", None),
        P("blk", None),
        P("blk", None),
    )
    return jax.shard_map(
        body, mesh=mesh, in_specs=placed, out_specs=P("blk", None, None), check_vma=False
    )
```

```python
import functools

import jax
import jax.numpy as jnp
import numpy as np
from jax import lax
from jax.experimental import pallas as pl
from jax.experimental.pallas import tpu as pltpu
from jax.sharding import PartitionSpec as P

MESH = pl.DeviceIdType.MESH
F32 = jnp.float32
BF16 = jnp.bfloat16
I32 = jnp.int32

VEL = [
    (0, 0, 0),
    (1, 0, 0),
    (-1, 0, 0),
    (0, 1, 0),
    (0, -1, 0),
    (0, 0, 1),
    (0, 0, -1),
    (1, 1, 0),
    (-1, -1, 0),
    (1, -1, 0),
    (-1, 1, 0),
    (1, 0, 1),
    (-1, 0, -1),
    (1, 0, -1),
    (-1, 0, 1),
    (0, 1, 1),
    (0, -1, -1),
    (0, 1, -1),
    (0, -1, 1),
]
OPP = [VEL.index((-x, -y, -z)) for x, y, z in VEL]
CROSS = [
    [q for q in range(19) if VEL[q][d // 2] == (-1 if d % 2 == 0 else 1)] for d in range(6)
]
BIT = [9 * (x + 1) + 3 * (y + 1) + (z + 1) for x, y, z in VEL]
OTHERS = [[q for q in range(19) if q not in CROSS[1 - d]] for d in range(2)]
BLK = 32
TILE = 128


def relax_delta(f):
    s = 1.0 / 0.6
    sx, dx = f[1] + f[2], f[1] - f[2]
    sy, dy = f[3] + f[4], f[3] - f[4]
    sz, dz = f[5] + f[6], f[5] - f[6]
    s7, d7 = f[7] + f[8], f[7] - f[8]
    s9, d9 = f[9] + f[10], f[9] - f[10]
    s11, d11 = f[11] + f[12], f[11] - f[12]
    s13, d13 = f[13] + f[14], f[13] - f[14]
    s15, d15 = f[15] + f[16], f[15] - f[16]
    s17, d17 = f[17] + f[18], f[17] - f[18]
    sa, ta = s7 + s9, s7 - s9
    sb, tb = s11 + s13, s11 - s13
    sc, tc = s15 + s17, s15 - s17
    ax, ay = d7 + d9, d7 - d9
    bx, bz = d11 + d13, d11 - d13
    cy, cz = d15 + d17, d15 - d17
    x2, mx = ax + bx, ax - bx
    y2, my = ay + cy, cy - ay
    z2, mz = bz + cz, bz - cz
    jx, jy, jz = dx + x2, dy + y2, dz + z2
    ab = sa + sb
    s2 = ab + sc
    yz = sy + sz
    s1 = sx + yz
    rho = f[0] + (s1 + s2)
    inv = 1.0 / rho
    ux, uy, uz = jx * inv, jy * inv, jz * inv
    xx, yy, zz = jx * ux, jy * uy, jz * uz
    jj = (xx + yy) + zz
    m1 = (s2 - f[0]) - jj
    m2 = 9.0 * f[0] - 7.0 * s1 - 2.0 * s2 + 5.5 * jj
    c1 = m1 * (19.0 * 1.19 / 2394.0)
    c2 = m2 * (1.4 / 252.0)
    a9 = (sx + sx) - yz
    b9 = ab - (sc + sc)
    e9 = (xx + xx) - (yy + zz)
    c9 = (a9 + b9 - e9) * (s / 36.0)
    c10 = (b9 - 2.0 * a9 + 0.5 * e9) * (1.4 / 72.0)
    a11 = sy - sz
    b11 = sa - sb
    e11 = yy - zz
    c11 = (a11 + b11 - e11) * (s / 12.0)
    c12 = (b11 - 2.0 * a11 + 0.5 * e11) * (1.4 / 24.0)
    c13 = (ta - jx * uy) * (s / 4.0)
    c14 = (tc - jy * uz) * (s / 4.0)
    c15 = (tb - jx * uz) * (s / 4.0)
    g = (5.0 / 3.0) * 1.2 / 40.0
    c4 = (x2 - 2.0 * dx) * g
    c6 = (y2 - 2.0 * dy) * g
    c8 = (z2 - 2.0 * dz) * g
    h = 1.98 / 8.0
    c16, c17, c18 = mx * h, my * h, mz * h
    r0 = 12.0 * c2 - 30.0 * c1
    ra = -11.0 * c1 - 4.0 * c2
    rd = 8.0 * c1 + c2
    p9 = c9 - 2.0 * c10
    p11 = c11 - 2.0 * c12
    n9 = c9 + c10
    n11 = c11 + c12
    ex = ra + 2.0 * p9
    et = ra - p9
    ey, ez = et + p11, et - p11
    rt = rd + n9
    exy, exz = rt + n11, rt - n11
    eyz = rd - 2.0 * n9
    ox, oy, oz = -4.0 * c4, -4.0 * c6, -4.0 * c8
    xa, ya = c4 + c16, c6 - c17
    xb, zb = c4 - c16, c8 + c18
    yc, zc = c6 + c17, c8 - c18
    e7, e9_ = exy + c13, exy - c13
    e11_, e13 = exz + c15, exz - c15
    e15, e17 = eyz + c14, eyz - c14
    o7, o9 = xa + ya, xa - ya
    o11, o13 = xb + zb, xb - zb
    o15, o17 = yc + zc, yc - zc
    out = [f[0] - r0]
    for q, even, odd in (
        (1, ex, ox),
        (3, ey, oy),
        (5, ez, oz),
        (7, e7, o7),
        (9, e9_, o9),
        (11, e11_, o11),
        (13, e13, o13),
        (15, e15, o15),
        (17, e17, o17),
    ):
        out.append(f[q] - (even + odd))
        out.append(f[q + 1] - (even - odd))
    return out


def split(x):
    hi = x.astype(BF16)
    lo = (x - hi.astype(F32)).astype(BF16)
    return jnp.concatenate([hi, lo], axis=0)


def roll(x, by):
    by %= TILE
    return pltpu.roll(x, by, 1) if by else x


def lanes():
    return lax.broadcasted_iota(I32, (BLK, TILE), 1)


def face_lanes(d, t, lane):
    if d == 0:
        return lane >= 64 if t == 3 else None
    if d == 1:
        return lane < 64 if t == 0 else None
    pos = ((lane >> 3) & 7) if d < 4 else (lane & 7)
    return pos == (7 if d % 2 == 0 else 0)


def cols(t):
    return pl.ds(t * TILE, TILE)


def pack_halves(vals, d, lane):
    keep = lane < 64 if d == 0 else lane >= 64
    tiles = []
    for s in range(0, len(vals), 2):
        tiles.append(jnp.where(keep, vals[s], roll(vals[s + 1], 64)))
    return tiles


def layer(ref, d, n):
    tile = ref[d, :, cols(n // 2)]
    return roll(tile, 64) if n % 2 else tile


def store_post(post, ref, packs, xs, key, t, lane):
    for q in range(19):
        ref[q, :, cols(t)] = post[q]
    low = lane & 7
    mid = (lane >> 3) & 7
    for d in range(2, 6):
        acc = post[CROSS[d][0]]
        for s in range(1, 5):
            step = (8 if d < 4 else 1) * s
            pos = mid if d < 4 else low
            by, at = (step, s) if d % 2 == 0 else (-step, 7 - s)
            acc = jnp.where(pos == at, roll(post[CROSS[d][s]], by), acc)
        packs[d - 2, :, cols(t)] = acc
    if t in (0, 3):
        d = 0 if t == 0 else 1
        vals = [post[q] for q in CROSS[d]] + [key]
        for s, tile in enumerate(pack_halves(vals, d, lane)):
            xs[d, :, cols(s)] = tile


def y_offset(d, s):
    return (56 - 8 * s) if d == 2 else (8 * s - 56)


def stream(ref, gh, gx, code_ref, t, lane, qs=tuple(range(19)), have=None):
    post = [ref[q, :, cols(t)] for q in range(19)]
    code = code_ref[:, cols(t)]
    upper = lane >= 64

    def merged(ex, here, load, edge):
        if ex == 0 or gx is None:
            return here
        near = t - ex
        other = load(near) if 0 <= near <= 3 else edge
        if other is None:
            return here
        return jnp.where(upper, other, here) if ex == 1 else jnp.where(upper, here, other)

    out = []
    for q in qs:
        if have and q in have:
            out.append(have[q])
            continue
        if q == 0:
            out.append(post[0])
            continue
        ex, ey, ez = VEL[q]
        edge = None
        if gx is not None and ex != 0 and not 0 <= t - ex <= 3:
            d = 0 if ex == -1 else 1
            edge = gx[d, CROSS[d].index(q), :, :]
        base = 64 * ex
        src = merged(ex, post[q], lambda u: ref[q, :, cols(u)], edge)
        moved = roll(src, base + 8 * ey + ez)
        for d, comp in ((2 if ey < 0 else 3, ey), (4 if ez < 0 else 5, ez)):
            if comp == 0:
                continue
            s = CROSS[d].index(q)
            if d < 4:
                off = y_offset(d, s) + base + ez
            else:
                off = (7 - s) * (1 if d == 4 else -1) + base + 8 * ey
            g = merged(ex, gh[d - 2, :, cols(t)], lambda u: gh[d - 2, :, cols(u)], None)
            moved = jnp.where(face_lanes(d, t, lane), roll(g, off), moved)
        usable = (code & (1 << BIT[q])) != 0
        out.append(jnp.where(usable, moved, post[OPP[q]]))
    return out


def far_edge(ref, d, g0, g1, ct, lane):
    t = 3 if d == 0 else 0
    cur = [None] * 19
    for n, q in enumerate(OTHERS[d]):
        cur[q] = layer(g1, d, n)
    for q in CROSS[1 - d]:
        ex, ey, ez = VEL[q]
        moved = roll(ref[q, :, cols(t)], 64 + 8 * ey + ez)
        back = layer(g0, d, CROSS[d].index(OPP[q]))
        for f, comp in ((2 if ey < 0 else 3, ey), (4 if ez < 0 else 5, ez)):
            if comp:
                moved = jnp.where(face_lanes(f, t, lane), back, moved)
        cur[q] = moved
    if d == 1:
        tile = g0[d, :, cols(2)]
        key = jnp.where(lane >= 64, roll(tile, 64), tile)
        group = ((lane & 63) >> 3).astype(F32)
        pick = jnp.where(key == group, 1.0, 0.0).astype(BF16)
        ghost = jnp.dot(pick, ct[...], preferred_element_type=F32)
        for s, q in enumerate(CROSS[2]):
            ex, ey, ez = VEL[q]
            if ex < 0:
                continue
            at = face_lanes(2, 3, lane) & (key >= 0.0)
            if ez:
                at = at & jnp.logical_not(face_lanes(4 if ez < 0 else 5, 3, lane))
            cur[q] = jnp.where(at, roll(ghost, y_offset(2, s) + 64 * ex + ez), cur[q])
    post = relax_delta(cur)
    return [post[q] for q in CROSS[d]]


def coarse_ghost(cfv, cs):
    ratio = 0.6 / 1.1
    cs[...] = jnp.zeros((2, 16, TILE), F32)
    row = lax.broadcasted_iota(I32, (2, 64), 0)
    w0 = jnp.where(row == 0, 0.0, 0.5)
    w1 = jnp.where(row == 0, 1.0, 0.5)

    def total(items):
        return functools.reduce(lambda a, b: a + b, items)

    for c in range(2):
        hs = []
        for q in range(19):
            both = cfv[c, q, :, :]
            hs.append(w1 * both + w0 * both[0:1, :])
        rho = total(hs)
        inv = 1.0 / rho
        vel = []
        for axis in range(3):
            plus = total([hs[q] for q in range(19) if VEL[q][axis] == 1])
            minus = total([hs[q] for q in range(19) if VEL[q][axis] == -1])
            vel.append((plus - minus) * inv)
        sq = 1.0 - 1.5 * (vel[0] * vel[0] + vel[1] * vel[1] + vel[2] * vel[2])
        for s, q in enumerate(CROSS[2]):
            proj = total(
                [v if e == 1 else -v for v, e in zip(vel, VEL[q]) if e]
            )
            weight = 1.0 / 18.0 if q < 7 else 1.0 / 36.0
            eq = (weight * rho) * (sq + 3.0 * proj + 4.5 * proj * proj)
            val = eq + ratio * (hs[q] - eq)
            for k in range(2):
                cs[k, pl.ds(8 * c + s, 1), 0:64] = val[k : k + 1, :]


def build_tables(me, nv, iv, pyz, pxl, pxr, pc, pw, rm, keys):
    row, col = (lax.broadcasted_iota(I32, (BLK, BLK), a) for a in (0, 1))
    eye = row == col

    def column(vals):
        wide = jnp.broadcast_to(vals.astype(F32), (BLK, BLK))
        return jnp.sum(jnp.where(eye, wide, 0.0), axis=1, keepdims=True)

    face = [column(nv[d : d + 1, :]) for d in range(6)]
    cb = column(iv[0:1, :])
    quad = column(iv[1:2, :])
    first = (me * BLK).astype(F32)
    slot = (lax.broadcasted_iota(I32, (BLK, 2 * BLK), 1) & (BLK - 1)).astype(F32)
    for d in range(6):
        local = jnp.where(face[d] >= 0.0, face[d] - first, -1.0)
        one = jnp.where(local == slot, 1.0, 0.0).astype(BF16)
        if d < 2:
            pxl[d] = one
            shift = -float(BLK) if d == 0 else float(BLK)
            there = jnp.where(face[d] >= 0.0, face[d] - first + shift, -1.0)
            pxr[d] = jnp.where(there == slot, 1.0, 0.0).astype(BF16)
            mine = (there >= 0.0) & (there < float(BLK))
            rm[d] = jnp.broadcast_to(jnp.where(mine, 1.0, 0.0), (BLK, TILE))
        else:
            pyz[d - 2] = one
    key = jnp.where(cb >= 0.0, 2.0 * quad + cb - 2.0 * (me + 1).astype(F32), -1.0)
    keys[...] = jnp.broadcast_to(key, (BLK, TILE))
    group = ((lax.broadcasted_iota(I32, (BLK, TILE), 1) & 63) >> 3).astype(F32)
    pc[...] = jnp.where(key == group, 1.0, 0.0).astype(BF16)
    for d in range(6):
        there = face[d] >= 0.0
        if d == 2:
            there = there | (cb >= 0.0)
        bits = sum(1 << BIT[q] for q in CROSS[d])
        pw[d] = jnp.broadcast_to(jnp.where(there, -1, ~bits), (BLK, TILE))


def build_code(sv, pw, code, lane):
    yz = []
    for t in range(4):
        fl = 1 - sv[:, cols(t)]
        wz = roll(fl, -1) | (fl << 1) | (roll(fl, 1) << 2)
        yz.append(roll(wz, -8) | (wz << 3) | (roll(wz, 8) << 6))
    ones = jnp.full((BLK, TILE), -1, I32)
    row = lax.broadcasted_iota(I32, (8, TILE), 1)
    for t in range(4):
        static = jnp.full((8, TILE), -1, I32)
        for q in range(7, 19):
            axes = [a for a in range(3) if VEL[q][a]]
            masks = [face_lanes(2 * a + (0 if VEL[q][a] < 0 else 1), t, row) for a in axes]
            if all(m is not None for m in masks):
                static = jnp.where(masks[0] & masks[1], static & ~(1 << BIT[q]), static)
        static = jnp.concatenate([static] * (BLK // 8), axis=0)
        below = yz[t - 1] if t > 0 else ones
        above = yz[t + 1] if t < 3 else ones
        up = roll(jnp.where(lane >= 64, below, yz[t]), 64) << 18
        down = roll(jnp.where(lane < 64, above, yz[t]), 64) & 511
        word = (up | (yz[t] << 9) | down) & static
        for d in range(6):
            m = face_lanes(d, t, lane)
            if m is not None:
                word = word & jnp.where(m, pw[d], -1)
        code[:, cols(t)] = word


def coarse_table(src, k, tiles):
    lane = lax.broadcasted_iota(I32, (8, TILE), 1)
    srow = lax.broadcasted_iota(I32, (8, TILE), 0)
    half = (lane & 7) >> 1
    at = (lane >> 3) & 7
    parts = []
    for quadrant in range(4):
        for c in range(2):
            vals = src[k, 8 * c : 8 * c + 8, :]
            wide = []
            for t in tiles:
                idx = half + (32 * (quadrant // 2) + 4 * (quadrant % 2) + 8 * t)
                got = jnp.take_along_axis(vals, idx, axis=1, mode="promise_in_bounds")
                wide.append(jnp.where(at == srow, got, 0.0))
            parts.append(jnp.concatenate(wide, axis=1))
    return split(jnp.concatenate(parts, axis=0))


def kernel(
    n,
    pops,
    coarse,
    nbr,
    itf,
    solid,
    out,
    f,
    pa,
    pb,
    packs,
    gh,
    g0,
    g1,
    gx,
    xs0,
    xr0,
    xs1,
    xr1,
    xl,
    cfv,
    nv,
    iv,
    sv,
    cs,
    cr,
    gc,
    code,
    pw,
    rm,
    keys,
    pyz,
    pxl,
    pxr,
    pc,
    ct,
    in_sem,
    send_sem,
    recv_sem,
):
    me = lax.axis_index("blk")
    peers = (lax.rem(me + n - 1, n), lax.rem(me + 1, n))
    has = (me > 0, me < n - 1)
    lane = lanes()
    barrier = pltpu.get_barrier_semaphore()

    def both(act):
        for k in range(2):
            pl.when(has[k])(functools.partial(act, k))

    def greet(k):
        pl.semaphore_signal(barrier, inc=1, device_id=(peers[k],), device_id_type=MESH)

    both(greet)

    def fetch(k, src, dst):
        c = pltpu.make_async_copy(src, dst, in_sem.at[k])
        c.start()
        return c

    def fetch_tiles(k, t, w=1):
        part = pl.ds(t * TILE, w * TILE)
        return fetch(k, pops.at[:, :, part], f.at[:, :, part])

    in_n = fetch(0, nbr, nv)
    in_i = fetch(1, itf, iv)
    in_c = fetch(2, coarse, cfv)
    in_s = fetch(3, solid, sv)
    in_3 = fetch_tiles(4, 3)
    in_0 = fetch_tiles(5, 0)
    in_m = fetch_tiles(6, 1, 2)

    def remote(sem, src, dst, k):
        return pltpu.make_async_remote_copy(
            src_ref=src,
            dst_ref=dst,
            send_sem=send_sem.at[sem],
            recv_sem=recv_sem.at[sem],
            device_id=(peers[k],),
            device_id_type=MESH,
        )

    def copy_a(k):
        return remote(k, xs0.at[k], xr0.at[k], k)

    def copy_b(k):
        return remote(2 + k, xs1.at[k], xr1.at[k], k)

    def copy_c():
        return remote(4, cs, cr, 0)

    def no_side(d):
        @pl.when(jnp.logical_not(has[1 - d]))
        def _():
            xr0[d] = jnp.zeros(xr0.shape[1:], F32)
            xr1[d] = jnp.zeros(xr1.shape[1:], F32)
            if d == 0:
                cr[...] = jnp.zeros(cr.shape, F32)

    for d in range(2):
        no_side(d)

    def first_collide(t):
        post = relax_delta([f[q, :, cols(t)] for q in range(19)])
        store_post(post, pa, packs, xs0, keys[...], t, lane)

    def second_collide(t, have=None):
        cur = stream(pa, gh.at[0], gx.at[0], code, t, lane, have=have)
        store_post(relax_delta(cur), pb, packs, xl, keys[...], t, lane)

    def finish(t):
        cur = stream(pb, gh.at[1], gx.at[1], code, t, lane)
        wet = (code[:, cols(t)] & (1 << BIT[0])) != 0
        for q in range(19):
            out[q, :, cols(t)] = jnp.where(wet, cur[q], f[q, :, cols(t)])

    def gather_tile(t, sub, coarse=True):
        for d in range(4):
            g = jnp.dot(pyz[d], split(packs[d, :, cols(t)]), preferred_element_type=F32)
            gh[sub, d, :, cols(t)] = g + gc[sub, :, cols(t)] if d == 0 and coarse else g

    def edge_stream(k):
        t = 3 if k == 1 else 0
        cur = stream(pa, gh.at[0], None, code, t, lane, qs=OTHERS[k])
        for s, tile in enumerate(pack_halves(cur, k, lane)):
            xs1[k, :, cols(s)] = tile
        return {q: v for q, v in zip(OTHERS[k], cur) if VEL[q][0] == 0}

    def local_x(d, src):
        return jnp.dot(pxl[d], split(src[d]), preferred_element_type=F32)

    def take_a(d):
        pl.when(has[1 - d])(lambda: copy_a(d).wait_recv())
        far = jnp.dot(pxr[d], split(xr0[d]), preferred_element_type=F32)
        g0[d] = g0[d] + far
        for s in range(5):
            gx[0, d, s] = layer(g0, d, s)

    def take_b(d):
        pl.when(has[1 - d])(lambda: copy_b(d).wait_recv())
        g1[d] = jnp.dot(pxr[d], split(xr1[d]), preferred_element_type=F32)
        vals = far_edge(pa, d, g0, g1, ct, lane)
        for s in range(5):
            gx[1, d, s] = vals[s]

    def join(d):
        near = local_x(d, xl)
        theirs = rm[d] != 0.0
        for s in range(5):
            tile = near[:, (s // 2) * TILE : (s // 2 + 1) * TILE]
            tile = roll(tile, 64) if s % 2 else tile
            gx[1, d, s] = jnp.where(theirs, gx[1, d, s], tile)

    in_n.wait()
    in_i.wait()
    build_tables(me, nv, iv, pyz, pxl, pxr, pc, pw, rm, keys)
    in_c.wait()
    coarse_ghost(cfv, cs)
    in_s.wait()
    build_code(sv, pw, code, lane)
    in_3.wait()
    first_collide(3)
    gather_tile(3, 0, coarse=False)
    have3 = edge_stream(1)
    for q in CROSS[2]:
        have3.pop(q, None)
    pl.semaphore_wait(barrier, has[0].astype(I32) + has[1].astype(I32))
    pl.when(has[0])(lambda: copy_c().start())

    @pl.when(has[1])
    def _():
        copy_a(1).start()
        copy_b(1).start()

    in_0.wait()
    first_collide(0)
    pl.when(has[0])(lambda: copy_a(0).start())
    in_m.wait()
    first_collide(1)
    first_collide(2)
    ct[...] = coarse_table(cs, 0, (3,))
    for d in range(2):
        g0[d] = local_x(d, xs0)

    pl.when(has[1])(lambda: copy_c().wait_recv())
    for k in range(2):
        gc[k] = jnp.dot(pc[...], coarse_table(cr, k, range(4)), preferred_element_type=F32)
    gather_tile(0, 0)
    have0 = edge_stream(0)
    pl.when(has[0])(lambda: copy_b(0).start())
    gather_tile(1, 0)
    gather_tile(2, 0)
    gh[0, 0, :, cols(3)] = gh[0, 0, :, cols(3)] + gc[0, :, cols(3)]
    second_collide(1)
    second_collide(2)

    def tail(near):
        far = 1 - near
        tile = {0: 3, 1: 0}
        mid = {0: 2, 1: 1}
        haves = {0: have3, 1: have0}
        take_a(near)
        second_collide(tile[near], haves[near])
        take_b(near)
        gather_tile(1, 1)
        gather_tile(2, 1)
        take_a(far)
        second_collide(tile[far], haves[far])
        gather_tile(3, 1)
        gather_tile(0, 1)
        finish(mid[near])
        join(near)
        finish(tile[near])
        finish(mid[far])
        take_b(far)
        join(far)
        finish(tile[far])

    is_even = lax.rem(me, 2) == 0
    pl.when(is_even)(lambda: tail(0))
    pl.when(jnp.logical_not(is_even))(lambda: tail(1))

    def drain(k):
        copy_a(k).wait_send()
        copy_b(k).wait_send()
        if k == 0:
            copy_c().wait_send()

    both(drain)


def body(populations, coarse_faces, neighbors, interface, solid):
    n = lax.axis_size("blk")
    pops = jnp.transpose(populations, (1, 0, 2))
    coarse = jnp.transpose(coarse_faces, (0, 2, 1, 3))
    ins = (pops, coarse, neighbors.T, interface.T, solid)
    ins = [pltpu.with_memory_space_constraint(v, pltpu.HBM) for v in ins]
    anywhere = pl.BlockSpec(memory_space=pl.ANY)
    vm = pltpu.VMEM
    big = vm((19, BLK, 512), F32)
    done = pl.pallas_call(
        functools.partial(kernel, n),
        out_shape=jax.ShapeDtypeStruct((19, BLK, 512), F32),
        in_specs=[anywhere] * 5,
        out_specs=pl.BlockSpec(memory_space=pltpu.VMEM),
        scratch_shapes=[
            big,
            big,
            big,
            vm((4, BLK, 512), F32),
            vm((2, 4, BLK, 512), F32),
            vm((2, BLK, 384), F32),
            vm((2, BLK, 896), F32),
            vm((2, 2, 5, BLK, TILE), F32),
            vm((2, BLK, 384), F32),
            vm((2, BLK, 384), F32),
            vm((2, BLK, 896), F32),
            vm((2, BLK, 896), F32),
            vm((2, BLK, 384), F32),
            vm((2, 19, 2, 64), F32),
            vm((6, BLK), I32),
            vm((2, BLK), I32),
            vm((BLK, 512), I32),
            vm((2, 16, TILE), F32),
            vm((2, 16, TILE), F32),
            vm((2, BLK, 512), F32),
            vm((BLK, 512), I32),
            vm((6, BLK, TILE), I32),
            vm((2, BLK, TILE), F32),
            vm((BLK, TILE), F32),
            vm((4, BLK, 2 * BLK), BF16),
            vm((2, BLK, 2 * BLK), BF16),
            vm((2, BLK, 2 * BLK), BF16),
            vm((BLK, TILE), BF16),
            vm((TILE, TILE), BF16),
            pltpu.SemaphoreType.DMA((7,)),
            pltpu.SemaphoreType.DMA((5,)),
            pltpu.SemaphoreType.DMA((5,)),
        ],
        compiler_params=pltpu.CompilerParams(
            collective_id=0, has_side_effects=True, vmem_limit_bytes=40 * 2**20
        ),
    )(*ins)
    return jnp.transpose(done, (1, 0, 2))


def solution(mesh):
    placed = (
        P("blk", None, None),
        P("blk", None, None, None),
        P("blk", None),
        P("blk", None),
        P("blk", None),
    )
    return jax.shard_map(
        body, mesh=mesh, in_specs=placed, out_specs=P("blk", None, None), check_vma=False
    )
```

```python
import functools

import jax
import jax.numpy as jnp
import numpy as np
from jax import lax
from jax.experimental import pallas as pl
from jax.experimental.pallas import tpu as pltpu
from jax.sharding import PartitionSpec as P

MESH = pl.DeviceIdType.MESH
F32 = jnp.float32
BF16 = jnp.bfloat16
I32 = jnp.int32

VEL = [
    (0, 0, 0),
    (1, 0, 0),
    (-1, 0, 0),
    (0, 1, 0),
    (0, -1, 0),
    (0, 0, 1),
    (0, 0, -1),
    (1, 1, 0),
    (-1, -1, 0),
    (1, -1, 0),
    (-1, 1, 0),
    (1, 0, 1),
    (-1, 0, -1),
    (1, 0, -1),
    (-1, 0, 1),
    (0, 1, 1),
    (0, -1, -1),
    (0, 1, -1),
    (0, -1, 1),
]
OPP = [VEL.index((-x, -y, -z)) for x, y, z in VEL]
CROSS = [
    [q for q in range(19) if VEL[q][d // 2] == (-1 if d % 2 == 0 else 1)] for d in range(6)
]
BIT = [9 * (x + 1) + 3 * (y + 1) + (z + 1) for x, y, z in VEL]
OTHERS = [
    [q for q in range(19) if q not in CROSS[1 - d] and q not in CROSS[2]]
    + [q for q in CROSS[2] if q not in CROSS[1 - d]]
    for d in range(2)
]
BLK = 32
TILE = 128
CHUNK = 16
CHUNKS = [slice(r, r + CHUNK) for r in range(0, BLK, CHUNK)]


def relax_delta(f):
    s = 1.0 / 0.6
    sx, dx = f[1] + f[2], f[1] - f[2]
    sy, dy = f[3] + f[4], f[3] - f[4]
    sz, dz = f[5] + f[6], f[5] - f[6]
    s7, d7 = f[7] + f[8], f[7] - f[8]
    s9, d9 = f[9] + f[10], f[9] - f[10]
    s11, d11 = f[11] + f[12], f[11] - f[12]
    s13, d13 = f[13] + f[14], f[13] - f[14]
    s15, d15 = f[15] + f[16], f[15] - f[16]
    s17, d17 = f[17] + f[18], f[17] - f[18]
    sa, ta = s7 + s9, s7 - s9
    sb, tb = s11 + s13, s11 - s13
    sc, tc = s15 + s17, s15 - s17
    ax, ay = d7 + d9, d7 - d9
    bx, bz = d11 + d13, d11 - d13
    cy, cz = d15 + d17, d15 - d17
    x2, mx = ax + bx, ax - bx
    y2, my = ay + cy, cy - ay
    z2, mz = bz + cz, bz - cz
    jx, jy, jz = dx + x2, dy + y2, dz + z2
    ab = sa + sb
    s2 = ab + sc
    yz = sy + sz
    s1 = sx + yz
    rho = f[0] + (s1 + s2)
    inv = 1.0 / rho
    ux, uy, uz = jx * inv, jy * inv, jz * inv
    xx, yy, zz = jx * ux, jy * uy, jz * uz
    jj = (xx + yy) + zz
    m1 = (s2 - f[0]) - jj
    m2 = 9.0 * f[0] - 7.0 * s1 - 2.0 * s2 + 5.5 * jj
    c1 = m1 * (19.0 * 1.19 / 2394.0)
    c2 = m2 * (1.4 / 252.0)
    a9 = (sx + sx) - yz
    b9 = ab - (sc + sc)
    e9 = (xx + xx) - (yy + zz)
    c9 = (a9 + b9 - e9) * (s / 36.0)
    c10 = (b9 - 2.0 * a9 + 0.5 * e9) * (1.4 / 72.0)
    a11 = sy - sz
    b11 = sa - sb
    e11 = yy - zz
    c11 = (a11 + b11 - e11) * (s / 12.0)
    c12 = (b11 - 2.0 * a11 + 0.5 * e11) * (1.4 / 24.0)
    c13 = (ta - jx * uy) * (s / 4.0)
    c14 = (tc - jy * uz) * (s / 4.0)
    c15 = (tb - jx * uz) * (s / 4.0)
    g = (5.0 / 3.0) * 1.2 / 40.0
    c4 = (x2 - 2.0 * dx) * g
    c6 = (y2 - 2.0 * dy) * g
    c8 = (z2 - 2.0 * dz) * g
    h = 1.98 / 8.0
    c16, c17, c18 = mx * h, my * h, mz * h
    r0 = 12.0 * c2 - 30.0 * c1
    ra = -11.0 * c1 - 4.0 * c2
    rd = 8.0 * c1 + c2
    p9 = c9 - 2.0 * c10
    p11 = c11 - 2.0 * c12
    n9 = c9 + c10
    n11 = c11 + c12
    ex = ra + 2.0 * p9
    et = ra - p9
    ey, ez = et + p11, et - p11
    rt = rd + n9
    exy, exz = rt + n11, rt - n11
    eyz = rd - 2.0 * n9
    ox, oy, oz = -4.0 * c4, -4.0 * c6, -4.0 * c8
    xa, ya = c4 + c16, c6 - c17
    xb, zb = c4 - c16, c8 + c18
    yc, zc = c6 + c17, c8 - c18
    e7, e9_ = exy + c13, exy - c13
    e11_, e13 = exz + c15, exz - c15
    e15, e17 = eyz + c14, eyz - c14
    o7, o9 = xa + ya, xa - ya
    o11, o13 = xb + zb, xb - zb
    o15, o17 = yc + zc, yc - zc
    out = [f[0] - r0]
    for q, even, odd in (
        (1, ex, ox),
        (3, ey, oy),
        (5, ez, oz),
        (7, e7, o7),
        (9, e9_, o9),
        (11, e11_, o11),
        (13, e13, o13),
        (15, e15, o15),
        (17, e17, o17),
    ):
        out.append(f[q] - (even + odd))
        out.append(f[q + 1] - (even - odd))
    return out


def split(x):
    hi = x.astype(BF16)
    lo = (x - hi.astype(F32)).astype(BF16)
    return jnp.concatenate([hi, lo], axis=0)


def roll(x, by):
    by %= TILE
    return pltpu.roll(x, by, 1) if by else x


def lanes():
    return lax.broadcasted_iota(I32, (CHUNK, TILE), 1)


def face_lanes(d, t, lane):
    if d == 0:
        return lane >= 64 if t == 3 else None
    if d == 1:
        return lane < 64 if t == 0 else None
    pos = ((lane >> 3) & 7) if d < 4 else (lane & 7)
    return pos == (7 if d % 2 == 0 else 0)


def cols(t):
    return pl.ds(t * TILE, TILE)


def pack_halves(vals, d, lane):
    keep = lane < 64 if d == 0 else lane >= 64
    tiles = []
    for s in range(0, len(vals), 2):
        tiles.append(jnp.where(keep, vals[s], roll(vals[s + 1], 64)))
    return tiles


def layer(ref, d, n, rs):
    tile = ref[d, rs, cols(n // 2)]
    return roll(tile, 64) if n % 2 else tile


def store_post(post, ref, packs, xs, key, t, lane, rs):
    for q in range(19):
        ref[q, rs, cols(t)] = post[q]
    low = lane & 7
    mid = (lane >> 3) & 7
    for d in range(2, 6):
        acc = post[CROSS[d][0]]
        for s in range(1, 5):
            step = (8 if d < 4 else 1) * s
            pos = mid if d < 4 else low
            by, at = (step, s) if d % 2 == 0 else (-step, 7 - s)
            acc = jnp.where(pos == at, roll(post[CROSS[d][s]], by), acc)
        packs[d - 2, rs, cols(t)] = acc
    if t in (0, 3):
        d = 0 if t == 0 else 1
        vals = [post[q] for q in CROSS[d]] + [key]
        for s, tile in enumerate(pack_halves(vals, d, lane)):
            xs[d, rs, cols(s)] = tile


def y_offset(d, s):
    return (56 - 8 * s) if d == 2 else (8 * s - 56)


def stream(ref, gh, gx, code_ref, t, lane, rs, qs=tuple(range(19)), have=None, alone=False):
    post = [ref[q, rs, cols(t)] for q in range(19)]
    code = code_ref[rs, cols(t)]
    upper = lane >= 64

    def merged(ex, here, load, edge):
        if ex == 0 or alone:
            return here
        near = t - ex
        other = load(near) if 0 <= near <= 3 else edge
        if other is None:
            return here
        return jnp.where(upper, other, here) if ex == 1 else jnp.where(upper, here, other)

    out = []
    for q in qs:
        if have and q in have:
            out.append(have[q])
            continue
        if q == 0:
            out.append(post[0])
            continue
        ex, ey, ez = VEL[q]
        edge = None
        if not alone and not 0 <= t - ex <= 3:
            d = 0 if ex == -1 else 1
            edge = gx[d, CROSS[d].index(q), rs, :]
        base = 64 * ex
        src = merged(ex, post[q], lambda u: ref[q, rs, cols(u)], edge)
        moved = roll(src, base + 8 * ey + ez)
        for d, comp in ((2 if ey < 0 else 3, ey), (4 if ez < 0 else 5, ez)):
            if comp == 0:
                continue
            s = CROSS[d].index(q)
            if d < 4:
                off = y_offset(d, s) + base + ez
            else:
                off = (7 - s) * (1 if d == 4 else -1) + base + 8 * ey
            g = merged(ex, gh[d - 2, rs, cols(t)], lambda u: gh[d - 2, rs, cols(u)], None)
            moved = jnp.where(face_lanes(d, t, lane), roll(g, off), moved)
        usable = (code & (1 << BIT[q])) != 0
        out.append(jnp.where(usable, moved, post[OPP[q]]))
    return out


def far_edge(ref, d, g0, g1, ghosts, lane, rs):
    t = 3 if d == 0 else 0
    cur = [None] * 19
    for n, q in enumerate(OTHERS[d]):
        cur[q] = layer(g1, d, n, rs)
    for q in CROSS[1 - d]:
        ex, ey, ez = VEL[q]
        moved = roll(ref[q, rs, cols(t)], 64 + 8 * ey + ez)
        back = layer(g0, d, CROSS[d].index(OPP[q]), rs)
        for f, comp in ((2 if ey < 0 else 3, ey), (4 if ez < 0 else 5, ez)):
            if comp:
                moved = jnp.where(face_lanes(f, t, lane), back, moved)
        cur[q] = moved
    if d == 1:
        key, ghost = ghosts[0][rs], ghosts[1][rs]
        for s, q in enumerate(CROSS[2]):
            ex, ey, ez = VEL[q]
            if ex < 0:
                continue
            at = face_lanes(2, 3, lane) & (key >= 0.0)
            if ez:
                at = at & jnp.logical_not(face_lanes(4 if ez < 0 else 5, 3, lane))
            cur[q] = jnp.where(at, roll(ghost, y_offset(2, s) + 64 * ex + ez), cur[q])
    post = relax_delta(cur)
    return [post[q] for q in CROSS[d]]


def their_coarse(g0, ct):
    tile = g0[1, :, cols(2)]
    lane = lax.broadcasted_iota(I32, (BLK, TILE), 1)
    key = jnp.where(lane >= 64, roll(tile, 64), tile)
    group = ((lane & 63) >> 3).astype(F32)
    pick = jnp.where(key == group, 1.0, 0.0).astype(BF16)
    return key, jnp.dot(pick, ct[...], preferred_element_type=F32)


def coarse_ghost(cfv, cs):
    ratio = 0.6 / 1.1
    cs[...] = jnp.zeros((2, 16, TILE), F32)
    row = lax.broadcasted_iota(I32, (2, 64), 0)
    w0 = jnp.where(row == 0, 0.0, 0.5)
    w1 = jnp.where(row == 0, 1.0, 0.5)

    def total(items):
        return functools.reduce(lambda a, b: a + b, items)

    for c in range(2):
        hs = []
        for q in range(19):
            both = cfv[c, q, :, :]
            hs.append(w1 * both + w0 * both[0:1, :])
        rho = total(hs)
        inv = 1.0 / rho
        vel = []
        for axis in range(3):
            plus = total([hs[q] for q in range(19) if VEL[q][axis] == 1])
            minus = total([hs[q] for q in range(19) if VEL[q][axis] == -1])
            vel.append((plus - minus) * inv)
        sq = 1.0 - 1.5 * (vel[0] * vel[0] + vel[1] * vel[1] + vel[2] * vel[2])
        for s, q in enumerate(CROSS[2]):
            proj = total(
                [v if e == 1 else -v for v, e in zip(vel, VEL[q]) if e]
            )
            weight = 1.0 / 18.0 if q < 7 else 1.0 / 36.0
            eq = (weight * rho) * (sq + 3.0 * proj + 4.5 * proj * proj)
            val = eq + ratio * (hs[q] - eq)
            for k in range(2):
                cs[k, pl.ds(8 * c + s, 1), 0:64] = val[k : k + 1, :]


def build_tables(me, nv, iv, pyz, pxl, pxr, pc, pw, rm, keys):
    row, col = (lax.broadcasted_iota(I32, (BLK, BLK), a) for a in (0, 1))
    eye = row == col

    def column(vals):
        wide = jnp.broadcast_to(vals.astype(F32), (BLK, BLK))
        return jnp.sum(jnp.where(eye, wide, 0.0), axis=1, keepdims=True)

    face = [column(nv[d : d + 1, :]) for d in range(6)]
    cb = column(iv[0:1, :])
    quad = column(iv[1:2, :])
    first = (me * BLK).astype(F32)
    slot = (lax.broadcasted_iota(I32, (BLK, 2 * BLK), 1) & (BLK - 1)).astype(F32)
    for d in range(6):
        local = jnp.where(face[d] >= 0.0, face[d] - first, -1.0)
        one = jnp.where(local == slot, 1.0, 0.0).astype(BF16)
        if d < 2:
            pxl[d] = one
            shift = -float(BLK) if d == 0 else float(BLK)
            there = jnp.where(face[d] >= 0.0, face[d] - first + shift, -1.0)
            pxr[d] = jnp.where(there == slot, 1.0, 0.0).astype(BF16)
            mine = (there >= 0.0) & (there < float(BLK))
            rm[d] = jnp.broadcast_to(jnp.where(mine, 1.0, 0.0), (BLK, TILE))
        else:
            pyz[d - 2] = one
    key = jnp.where(cb >= 0.0, 2.0 * quad + cb - 2.0 * (me + 1).astype(F32), -1.0)
    keys[...] = jnp.broadcast_to(key, (BLK, TILE))
    group = ((lax.broadcasted_iota(I32, (BLK, TILE), 1) & 63) >> 3).astype(F32)
    pc[...] = jnp.where(key == group, 1.0, 0.0).astype(BF16)
    for d in range(6):
        there = face[d] >= 0.0
        if d == 2:
            there = there | (cb >= 0.0)
        bits = sum(1 << BIT[q] for q in CROSS[d])
        pw[d] = jnp.broadcast_to(jnp.where(there, -1, ~bits), (BLK, TILE))


def build_code(sv, pw, code, lane, rs):
    yz = []
    for t in range(4):
        fl = 1 - sv[rs, cols(t)]
        wz = roll(fl, -1) | (fl << 1) | (roll(fl, 1) << 2)
        yz.append(roll(wz, -8) | (wz << 3) | (roll(wz, 8) << 6))
    ones = jnp.full((CHUNK, TILE), -1, I32)
    row = lax.broadcasted_iota(I32, (8, TILE), 1)
    for t in range(4):
        static = jnp.full((8, TILE), -1, I32)
        for q in range(7, 19):
            axes = [a for a in range(3) if VEL[q][a]]
            masks = [face_lanes(2 * a + (0 if VEL[q][a] < 0 else 1), t, row) for a in axes]
            if all(m is not None for m in masks):
                static = jnp.where(masks[0] & masks[1], static & ~(1 << BIT[q]), static)
        static = jnp.concatenate([static] * (CHUNK // 8), axis=0)
        below = yz[t - 1] if t > 0 else ones
        above = yz[t + 1] if t < 3 else ones
        up = roll(jnp.where(lane >= 64, below, yz[t]), 64) << 18
        down = roll(jnp.where(lane < 64, above, yz[t]), 64) & 511
        word = (up | (yz[t] << 9) | down) & static
        for d in range(6):
            m = face_lanes(d, t, lane)
            if m is not None:
                word = word & jnp.where(m, pw[d, rs, :], -1)
        code[rs, cols(t)] = word


def coarse_table(src, k, tiles):
    lane = lax.broadcasted_iota(I32, (8, TILE), 1)
    srow = lax.broadcasted_iota(I32, (8, TILE), 0)
    half = (lane & 7) >> 1
    at = (lane >> 3) & 7
    parts = []
    for quadrant in range(4):
        for c in range(2):
            vals = src[k, 8 * c : 8 * c + 8, :]
            wide = []
            for t in tiles:
                idx = half + (32 * (quadrant // 2) + 4 * (quadrant % 2) + 8 * t)
                got = jnp.take_along_axis(vals, idx, axis=1, mode="promise_in_bounds")
                wide.append(jnp.where(at == srow, got, 0.0))
            parts.append(jnp.concatenate(wide, axis=1))
    return split(jnp.concatenate(parts, axis=0))


def kernel(
    n,
    pops,
    coarse,
    nbr,
    itf,
    solid,
    out,
    f,
    pa,
    pb,
    packs,
    gh,
    g0,
    g1,
    gx,
    xs0,
    xr0,
    xs1,
    xr1,
    xl,
    cfv,
    nv,
    iv,
    sv,
    cs,
    cr,
    gc,
    code,
    pw,
    rm,
    keys,
    pyz,
    pxl,
    pxr,
    pc,
    ct,
    in_sem,
    send_sem,
    recv_sem,
):
    me = lax.axis_index("blk")
    peers = (lax.rem(me + n - 1, n), lax.rem(me + 1, n))
    has = (me > 0, me < n - 1)
    lane = lanes()
    barrier = pltpu.get_barrier_semaphore()

    def both(act):
        for k in range(2):
            pl.when(has[k])(functools.partial(act, k))

    def greet(k):
        pl.semaphore_signal(barrier, inc=1, device_id=(peers[k],), device_id_type=MESH)

    both(greet)

    def fetch(k, src, dst):
        c = pltpu.make_async_copy(src, dst, in_sem.at[k])
        c.start()
        return c

    def fetch_tiles(k, t, w=1):
        part = pl.ds(t * TILE, w * TILE)
        return fetch(k, pops.at[:, :, part], f.at[:, :, part])

    in_n = fetch(0, nbr, nv)
    in_i = fetch(1, itf, iv)
    in_c = fetch(2, coarse, cfv)
    in_s = fetch(3, solid, sv)
    in_3 = fetch_tiles(4, 3)
    in_0 = fetch_tiles(5, 0)
    in_m = fetch_tiles(6, 1, 2)

    def remote(sem, src, dst, k):
        return pltpu.make_async_remote_copy(
            src_ref=src,
            dst_ref=dst,
            send_sem=send_sem.at[sem],
            recv_sem=recv_sem.at[sem],
            device_id=(peers[k],),
            device_id_type=MESH,
        )

    def copy_a(k):
        return remote(k, xs0.at[k], xr0.at[k], k)

    def copy_b(k):
        return remote(2 + k, xs1.at[k], xr1.at[k], k)

    def copy_c():
        return remote(4, cs, cr, 0)

    def no_side(d):
        @pl.when(jnp.logical_not(has[1 - d]))
        def _():
            xr0[d] = jnp.zeros(xr0.shape[1:], F32)
            xr1[d] = jnp.zeros(xr1.shape[1:], F32)
            if d == 0:
                cr[...] = jnp.zeros(cr.shape, F32)

    for d in range(2):
        no_side(d)

    def first_collide(t):
        for rs in CHUNKS:
            post = relax_delta([f[q, rs, cols(t)] for q in range(19)])
            store_post(post, pa, packs, xs0, keys[rs, :], t, lane, rs)

    def second_collide(t):
        for n, rs in enumerate(CHUNKS):
            cur = stream(pa, gh.at[0], gx.at[0], code, t, lane, rs, have=have[t][n])
            store_post(relax_delta(cur), pb, packs, xl, keys[rs, :], t, lane, rs)

    have = [[{} for _ in CHUNKS] for _ in range(4)]

    def early(t, qs):
        for n, rs in enumerate(CHUNKS):
            qs = [q for q in qs if q not in have[t][n]]
            cur = stream(pa, gh.at[0], gx.at[0], code, t, lane, rs, qs=qs)
            have[t][n].update(zip(qs, cur))

    def finish(t):
        for rs in CHUNKS:
            cur = stream(pb, gh.at[1], gx.at[1], code, t, lane, rs)
            wet = (code[rs, cols(t)] & (1 << BIT[0])) != 0
            for q in range(19):
                out[q, rs, cols(t)] = jnp.where(wet, cur[q], f[q, rs, cols(t)])

    def gather_tile(t, sub, coarse=True):
        for d in range(4):
            g = jnp.dot(pyz[d], split(packs[d, :, cols(t)]), preferred_element_type=F32)
            gh[sub, d, :, cols(t)] = g + gc[sub, :, cols(t)] if d == 0 and coarse else g

    def edge_stream(k, part):
        t = 3 if k == 1 else 0
        qs = OTHERS[k][part]
        for n, rs in enumerate(CHUNKS):
            cur = stream(
                pa, gh.at[0], None, code, t, lane, rs, qs=qs, have=have[t][n], alone=True
            )
            for s, tile in enumerate(pack_halves(cur, k, lane)):
                xs1[k, rs, cols((part.start or 0) // 2 + s)] = tile
            for q, v in zip(qs, cur):
                if VEL[q][0] == 0 and (k == 0 or q not in CROSS[2]):
                    have[t][n][q] = v

    def local_x(d, src):
        return jnp.dot(pxl[d], split(src[d]), preferred_element_type=F32)

    def take_a(d):
        pl.when(has[1 - d])(lambda: copy_a(d).wait_recv())
        far = jnp.dot(pxr[d], split(xr0[d]), preferred_element_type=F32)
        g0[d] = g0[d] + far
        for s in range(5):
            gx[0, d, s] = layer(g0, d, s, slice(None))

    def take_b(d):
        pl.when(has[1 - d])(lambda: copy_b(d).wait_recv())
        g1[d] = jnp.dot(pxr[d], split(xr1[d]), preferred_element_type=F32)
        ghosts = their_coarse(g0, ct) if d == 1 else None
        for rs in CHUNKS:
            vals = far_edge(pa, d, g0, g1, ghosts, lane, rs)
            for s in range(5):
                gx[1, d, s, rs, :] = vals[s]

    def join(d):
        near = local_x(d, xl)
        theirs = rm[d] != 0.0
        for s in range(5):
            tile = near[:, (s // 2) * TILE : (s // 2 + 1) * TILE]
            tile = roll(tile, 64) if s % 2 else tile
            gx[1, d, s] = jnp.where(theirs, gx[1, d, s], tile)

    def coarse_fine(k):
        gc[k] = jnp.dot(pc[...], coarse_table(cr, k, range(4)), preferred_element_type=F32)

    in_n.wait()
    in_i.wait()
    build_tables(me, nv, iv, pyz, pxl, pxr, pc, pw, rm, keys)
    in_c.wait()
    coarse_ghost(cfv, cs)
    in_s.wait()
    for rs in CHUNKS:
        build_code(sv, pw, code, lane, rs)
    in_3.wait()
    first_collide(3)
    gather_tile(3, 0, coarse=False)
    edge_stream(1, slice(None))
    pl.semaphore_wait(barrier, has[0].astype(I32) + has[1].astype(I32))
    pl.when(has[0])(lambda: copy_c().start())

    @pl.when(has[1])
    def _():
        copy_a(1).start()
        copy_b(1).start()

    in_0.wait()
    first_collide(0)
    pl.when(has[0])(lambda: copy_a(0).start())
    in_m.wait()
    first_collide(1)
    first_collide(2)
    ct[...] = coarse_table(cs, 0, (3,))
    for d in range(2):
        g0[d] = local_x(d, xs0)
    for t in range(3):
        gather_tile(t, 0, coarse=False)
    edge_stream(0, slice(0, 10))
    dry = [q for q in range(19) if q not in CROSS[2]]
    early(0, [q for q in dry if VEL[q][0] != 1])
    early(1, dry)
    early(2, dry)
    early(3, [q for q in dry if VEL[q][0] != -1])

    pl.when(has[1])(lambda: copy_c().wait_recv())
    coarse_fine(0)
    gh[0, 0] = gh[0, 0] + gc[0]
    edge_stream(0, slice(10, 14))
    pl.when(has[0])(lambda: copy_b(0).start())
    second_collide(1)
    second_collide(2)
    coarse_fine(1)

    def tail(near):
        far = 1 - near
        tile = {0: 3, 1: 0}
        mid = {0: 2, 1: 1}
        take_a(near)
        second_collide(tile[near])
        take_b(near)
        gather_tile(1, 1)
        gather_tile(2, 1)
        take_a(far)
        second_collide(tile[far])
        gather_tile(3, 1)
        gather_tile(0, 1)
        finish(mid[near])
        join(near)
        finish(tile[near])
        finish(mid[far])
        take_b(far)
        join(far)
        finish(tile[far])

    is_even = lax.rem(me, 2) == 0
    pl.when(is_even)(lambda: tail(0))
    pl.when(jnp.logical_not(is_even))(lambda: tail(1))

    def drain(k):
        copy_a(k).wait_send()
        copy_b(k).wait_send()
        if k == 0:
            copy_c().wait_send()

    both(drain)


def body(populations, coarse_faces, neighbors, interface, solid):
    n = lax.axis_size("blk")
    pops = jnp.transpose(populations, (1, 0, 2))
    coarse = jnp.transpose(coarse_faces, (0, 2, 1, 3))
    ins = (pops, coarse, neighbors.T, interface.T, solid)
    ins = [pltpu.with_memory_space_constraint(v, pltpu.HBM) for v in ins]
    anywhere = pl.BlockSpec(memory_space=pl.ANY)
    vm = pltpu.VMEM
    big = vm((19, BLK, 512), F32)
    done = pl.pallas_call(
        functools.partial(kernel, n),
        out_shape=jax.ShapeDtypeStruct((19, BLK, 512), F32),
        in_specs=[anywhere] * 5,
        out_specs=pl.BlockSpec(memory_space=pltpu.VMEM),
        scratch_shapes=[
            big,
            big,
            big,
            vm((4, BLK, 512), F32),
            vm((2, 4, BLK, 512), F32),
            vm((2, BLK, 384), F32),
            vm((2, BLK, 896), F32),
            vm((2, 2, 5, BLK, TILE), F32),
            vm((2, BLK, 384), F32),
            vm((2, BLK, 384), F32),
            vm((2, BLK, 896), F32),
            vm((2, BLK, 896), F32),
            vm((2, BLK, 384), F32),
            vm((2, 19, 2, 64), F32),
            vm((6, BLK), I32),
            vm((2, BLK), I32),
            vm((BLK, 512), I32),
            vm((2, 16, TILE), F32),
            vm((2, 16, TILE), F32),
            vm((2, BLK, 512), F32),
            vm((BLK, 512), I32),
            vm((6, BLK, TILE), I32),
            vm((2, BLK, TILE), F32),
            vm((BLK, TILE), F32),
            vm((4, BLK, 2 * BLK), BF16),
            vm((2, BLK, 2 * BLK), BF16),
            vm((2, BLK, 2 * BLK), BF16),
            vm((BLK, TILE), BF16),
            vm((TILE, TILE), BF16),
            pltpu.SemaphoreType.DMA((7,)),
            pltpu.SemaphoreType.DMA((5,)),
            pltpu.SemaphoreType.DMA((5,)),
        ],
        compiler_params=pltpu.CompilerParams(
            collective_id=0, has_side_effects=True, vmem_limit_bytes=40 * 2**20
        ),
    )(*ins)
    return jnp.transpose(done, (1, 0, 2))


def solution(mesh):
    placed = (
        P("blk", None, None),
        P("blk", None, None, None),
        P("blk", None),
        P("blk", None),
        P("blk", None),
    )
    return jax.shard_map(
        body, mesh=mesh, in_specs=placed, out_specs=P("blk", None, None), check_vma=False
    )
```

```python
import functools

import jax
import jax.numpy as jnp
import numpy as np
from jax import lax
from jax.experimental import pallas as pl
from jax.experimental.pallas import tpu as pltpu
from jax.sharding import PartitionSpec as P

MESH = pl.DeviceIdType.MESH
F32 = jnp.float32
BF16 = jnp.bfloat16
I32 = jnp.int32

VEL = [
    (0, 0, 0),
    (1, 0, 0),
    (-1, 0, 0),
    (0, 1, 0),
    (0, -1, 0),
    (0, 0, 1),
    (0, 0, -1),
    (1, 1, 0),
    (-1, -1, 0),
    (1, -1, 0),
    (-1, 1, 0),
    (1, 0, 1),
    (-1, 0, -1),
    (1, 0, -1),
    (-1, 0, 1),
    (0, 1, 1),
    (0, -1, -1),
    (0, 1, -1),
    (0, -1, 1),
]
OPP = [VEL.index((-x, -y, -z)) for x, y, z in VEL]
CROSS = [
    [q for q in range(19) if VEL[q][d // 2] == (-1 if d % 2 == 0 else 1)] for d in range(6)
]
BIT = [9 * (x + 1) + 3 * (y + 1) + (z + 1) for x, y, z in VEL]
OTHERS = [
    [q for q in range(19) if q not in CROSS[1 - d] and q not in CROSS[2]]
    + [q for q in CROSS[2] if q not in CROSS[1 - d]]
    for d in range(2)
]
BLK = 32
TILE = 128
CHUNK = 16
CHUNKS = [slice(r, r + CHUNK) for r in range(0, BLK, CHUNK)]


def relax_delta(f):
    s = 1.0 / 0.6
    sx, dx = f[1] + f[2], f[1] - f[2]
    sy, dy = f[3] + f[4], f[3] - f[4]
    sz, dz = f[5] + f[6], f[5] - f[6]
    s7, d7 = f[7] + f[8], f[7] - f[8]
    s9, d9 = f[9] + f[10], f[9] - f[10]
    s11, d11 = f[11] + f[12], f[11] - f[12]
    s13, d13 = f[13] + f[14], f[13] - f[14]
    s15, d15 = f[15] + f[16], f[15] - f[16]
    s17, d17 = f[17] + f[18], f[17] - f[18]
    sa, ta = s7 + s9, s7 - s9
    sb, tb = s11 + s13, s11 - s13
    sc, tc = s15 + s17, s15 - s17
    ax, ay = d7 + d9, d7 - d9
    bx, bz = d11 + d13, d11 - d13
    cy, cz = d15 + d17, d15 - d17
    x2, mx = ax + bx, ax - bx
    y2, my = ay + cy, cy - ay
    z2, mz = bz + cz, bz - cz
    jx, jy, jz = dx + x2, dy + y2, dz + z2
    ab = sa + sb
    s2 = ab + sc
    yz = sy + sz
    s1 = sx + yz
    rho = f[0] + (s1 + s2)
    inv = 1.0 / rho
    ux, uy, uz = jx * inv, jy * inv, jz * inv
    xx, yy, zz = jx * ux, jy * uy, jz * uz
    jj = (xx + yy) + zz
    m1 = (s2 - f[0]) - jj
    m2 = 9.0 * f[0] - 7.0 * s1 - 2.0 * s2 + 5.5 * jj
    c1 = m1 * (19.0 * 1.19 / 2394.0)
    c2 = m2 * (1.4 / 252.0)
    a9 = (sx + sx) - yz
    b9 = ab - (sc + sc)
    e9 = (xx + xx) - (yy + zz)
    c9 = (a9 + b9 - e9) * (s / 36.0)
    c10 = (b9 - 2.0 * a9 + 0.5 * e9) * (1.4 / 72.0)
    a11 = sy - sz
    b11 = sa - sb
    e11 = yy - zz
    c11 = (a11 + b11 - e11) * (s / 12.0)
    c12 = (b11 - 2.0 * a11 + 0.5 * e11) * (1.4 / 24.0)
    c13 = (ta - jx * uy) * (s / 4.0)
    c14 = (tc - jy * uz) * (s / 4.0)
    c15 = (tb - jx * uz) * (s / 4.0)
    g = (5.0 / 3.0) * 1.2 / 40.0
    c4 = (x2 - 2.0 * dx) * g
    c6 = (y2 - 2.0 * dy) * g
    c8 = (z2 - 2.0 * dz) * g
    h = 1.98 / 8.0
    c16, c17, c18 = mx * h, my * h, mz * h
    r0 = 12.0 * c2 - 30.0 * c1
    ra = -11.0 * c1 - 4.0 * c2
    rd = 8.0 * c1 + c2
    p9 = c9 - 2.0 * c10
    p11 = c11 - 2.0 * c12
    n9 = c9 + c10
    n11 = c11 + c12
    ex = ra + 2.0 * p9
    et = ra - p9
    ey, ez = et + p11, et - p11
    rt = rd + n9
    exy, exz = rt + n11, rt - n11
    eyz = rd - 2.0 * n9
    ox, oy, oz = -4.0 * c4, -4.0 * c6, -4.0 * c8
    xa, ya = c4 + c16, c6 - c17
    xb, zb = c4 - c16, c8 + c18
    yc, zc = c6 + c17, c8 - c18
    e7, e9_ = exy + c13, exy - c13
    e11_, e13 = exz + c15, exz - c15
    e15, e17 = eyz + c14, eyz - c14
    o7, o9 = xa + ya, xa - ya
    o11, o13 = xb + zb, xb - zb
    o15, o17 = yc + zc, yc - zc
    out = [f[0] - r0]
    for q, even, odd in (
        (1, ex, ox),
        (3, ey, oy),
        (5, ez, oz),
        (7, e7, o7),
        (9, e9_, o9),
        (11, e11_, o11),
        (13, e13, o13),
        (15, e15, o15),
        (17, e17, o17),
    ):
        out.append(f[q] - (even + odd))
        out.append(f[q + 1] - (even - odd))
    return out


def split(x):
    hi = x.astype(BF16)
    lo = (x - hi.astype(F32)).astype(BF16)
    return jnp.concatenate([hi, lo], axis=0)


def roll(x, by):
    by %= TILE
    return pltpu.roll(x, by, 1) if by else x


def lanes():
    return lax.broadcasted_iota(I32, (CHUNK, TILE), 1)


def face_lanes(d, t, lane):
    if d == 0:
        return lane >= 64 if t == 3 else None
    if d == 1:
        return lane < 64 if t == 0 else None
    pos = ((lane >> 3) & 7) if d < 4 else (lane & 7)
    return pos == (7 if d % 2 == 0 else 0)


def cols(t):
    return pl.ds(t * TILE, TILE)


def pack_halves(vals, d, lane):
    keep = lane < 64 if d == 0 else lane >= 64
    tiles = []
    for s in range(0, len(vals), 2):
        tiles.append(jnp.where(keep, vals[s], roll(vals[s + 1], 64)))
    return tiles


def layer(ref, d, n, rs):
    tile = ref[d, rs, cols(n // 2)]
    return roll(tile, 64) if n % 2 else tile


def store_post(post, ref, packs, xs, key, t, lane, rs):
    for q in range(19):
        ref[q, rs, cols(t)] = post[q]
    first = [face_lanes(3, t, lane), face_lanes(5, t, lane)]
    for h in range(2):
        for n in range(5):
            a, b = CROSS[2 + 2 * h][n], CROSS[3 + 2 * h][n]
            packs[5 * h + n, rs, cols(t)] = jnp.where(first[h], post[a], post[b])
    if t in (0, 3):
        d = 0 if t == 0 else 1
        vals = [post[q] for q in CROSS[d]] + [key]
        for s, tile in enumerate(pack_halves(vals, d, lane)):
            xs[d, rs, cols(s)] = tile


def stream(ref, gh, gx, code_ref, t, lane, rs, qs=tuple(range(19)), have=None, alone=False):
    post = [ref[q, rs, cols(t)] for q in range(19)]
    code = code_ref[rs, cols(t)]
    upper = lane >= 64

    def merged(ex, here, load, edge):
        if ex == 0 or alone:
            return here
        near = t - ex
        other = load(near) if 0 <= near <= 3 else edge
        if other is None:
            return here
        return jnp.where(upper, other, here) if ex == 1 else jnp.where(upper, here, other)

    out = []
    for q in qs:
        if have and q in have:
            out.append(have[q])
            continue
        if q == 0:
            out.append(post[0])
            continue
        ex, ey, ez = VEL[q]
        edge = None
        if not alone and not 0 <= t - ex <= 3:
            d = 0 if ex == -1 else 1
            edge = gx[d, CROSS[d].index(q), rs, :]
        src = merged(ex, post[q], lambda u: ref[q, rs, cols(u)], edge)

        def ghost(n, at):
            here = gh[n, rs, cols(t)]
            if ex == 0 or alone or not 0 <= t - ex <= 3:
                return here
            other = gh[n, rs, cols(t - ex)]
            return jnp.where(at, other, here) if ex == 1 else jnp.where(at, here, other)

        if ey:
            d = 2 if ey < 0 else 3
            g = ghost(CROSS[d].index(q), jnp.logical_not(upper))
            src = jnp.where(face_lanes(d ^ 1, t, lane), g, src)
        if ez:
            d = 4 if ez < 0 else 5
            wrapped = face_lanes(3 if ez < 0 else 2, t, lane)
            g = ghost(5 + CROSS[d].index(q), jnp.logical_xor(upper, wrapped))
            src = jnp.where(face_lanes(d ^ 1, t, lane), g, src)
        moved = roll(src, 64 * ex + 8 * ey + ez)
        usable = (code & (1 << BIT[q])) != 0
        out.append(jnp.where(usable, moved, post[OPP[q]]))
    return out


def far_edge(ref, d, g0, g1, ghosts, lane, rs):
    t = 3 if d == 0 else 0
    cur = [None] * 19
    for n, q in enumerate(OTHERS[d]):
        cur[q] = layer(g1, d, n, rs)
    for q in CROSS[1 - d]:
        ex, ey, ez = VEL[q]
        moved = roll(ref[q, rs, cols(t)], 64 + 8 * ey + ez)
        back = layer(g0, d, CROSS[d].index(OPP[q]), rs)
        for f, comp in ((2 if ey < 0 else 3, ey), (4 if ez < 0 else 5, ez)):
            if comp:
                moved = jnp.where(face_lanes(f, t, lane), back, moved)
        cur[q] = moved
    if d == 1:
        key = ghosts[0][rs]
        ghost = [g[rs] for g in ghosts[1]]
        for s, q in enumerate(CROSS[2]):
            ex, ey, ez = VEL[q]
            if ex < 0:
                continue
            at = face_lanes(2, 3, lane) & (key >= 0.0)
            if ez:
                at = at & jnp.logical_not(face_lanes(4 if ez < 0 else 5, 3, lane))
            cur[q] = jnp.where(at, roll(ghost[s], ez), cur[q])
    post = relax_delta(cur)
    return [post[q] for q in CROSS[d]]


def their_coarse(g0, ct):
    tile = g0[1, :, cols(2)]
    lane = lax.broadcasted_iota(I32, (BLK, TILE), 1)
    key = jnp.where(lane >= 64, roll(tile, 64), tile)
    out = jnp.dot(coarse_pick(key, lane), ct[...], preferred_element_type=F32)
    return key, [out[BLK * n : BLK * (n + 1)] for n in range(5)]


def coarse_pick(key, lane):
    group = ((lane & 63) >> 3).astype(F32)
    mine = key == group
    rows = [jnp.where(mine & ((lane & 7) == n), 1.0, 0.0) for n in range(5)]
    return jnp.concatenate(rows, axis=0).astype(BF16)


def coarse_ghost(cfv, cs):
    ratio = 0.6 / 1.1
    cs[...] = jnp.zeros((2, 16, TILE), F32)
    row = lax.broadcasted_iota(I32, (2, 64), 0)
    w0 = jnp.where(row == 0, 0.0, 0.5)
    w1 = jnp.where(row == 0, 1.0, 0.5)

    def total(items):
        return functools.reduce(lambda a, b: a + b, items)

    for c in range(2):
        hs = []
        for q in range(19):
            both = cfv[c, q, :, :]
            hs.append(w1 * both + w0 * both[0:1, :])
        rho = total(hs)
        inv = 1.0 / rho
        vel = []
        for axis in range(3):
            plus = total([hs[q] for q in range(19) if VEL[q][axis] == 1])
            minus = total([hs[q] for q in range(19) if VEL[q][axis] == -1])
            vel.append((plus - minus) * inv)
        sq = 1.0 - 1.5 * (vel[0] * vel[0] + vel[1] * vel[1] + vel[2] * vel[2])
        for s, q in enumerate(CROSS[2]):
            proj = total(
                [v if e == 1 else -v for v, e in zip(vel, VEL[q]) if e]
            )
            weight = 1.0 / 18.0 if q < 7 else 1.0 / 36.0
            eq = (weight * rho) * (sq + 3.0 * proj + 4.5 * proj * proj)
            val = eq + ratio * (hs[q] - eq)
            for k in range(2):
                cs[k, pl.ds(8 * c + s, 1), 0:64] = val[k : k + 1, :]


def build_tables(me, nv, iv, pyz, pxl, pxr, pc, pw, rm, keys):
    row, col = (lax.broadcasted_iota(I32, (BLK, BLK), a) for a in (0, 1))
    eye = row == col

    def column(vals):
        wide = jnp.broadcast_to(vals.astype(F32), (BLK, BLK))
        return jnp.sum(jnp.where(eye, wide, 0.0), axis=1, keepdims=True)

    face = [column(nv[d : d + 1, :]) for d in range(6)]
    cb = column(iv[0:1, :])
    quad = column(iv[1:2, :])
    first = (me * BLK).astype(F32)
    slot = (lax.broadcasted_iota(I32, (BLK, 2 * BLK), 1) & (BLK - 1)).astype(F32)
    for d in range(6):
        local = jnp.where(face[d] >= 0.0, face[d] - first, -1.0)
        one = jnp.where(local == slot, 1.0, 0.0).astype(BF16)
        if d < 2:
            pxl[d] = one
            shift = -float(BLK) if d == 0 else float(BLK)
            there = jnp.where(face[d] >= 0.0, face[d] - first + shift, -1.0)
            pxr[d] = jnp.where(there == slot, 1.0, 0.0).astype(BF16)
            mine = (there >= 0.0) & (there < float(BLK))
            rm[d] = jnp.broadcast_to(jnp.where(mine, 1.0, 0.0), (BLK, TILE))
        else:
            pyz[d // 2 - 1, BLK * (d % 2) : BLK * (d % 2 + 1)] = one
    key = jnp.where(cb >= 0.0, 2.0 * quad + cb - 2.0 * (me + 1).astype(F32), -1.0)
    keys[...] = jnp.broadcast_to(key, (BLK, TILE))
    pc[...] = coarse_pick(key, lax.broadcasted_iota(I32, (BLK, TILE), 1))
    for d in range(6):
        there = face[d] >= 0.0
        if d == 2:
            there = there | (cb >= 0.0)
        bits = sum(1 << BIT[q] for q in CROSS[d])
        pw[d] = jnp.broadcast_to(jnp.where(there, -1, ~bits), (BLK, TILE))


def build_code(sv, pw, code, lane, rs):
    yz = []
    for t in range(4):
        fl = 1 - sv[rs, cols(t)]
        wz = roll(fl, -1) | (fl << 1) | (roll(fl, 1) << 2)
        yz.append(roll(wz, -8) | (wz << 3) | (roll(wz, 8) << 6))
    ones = jnp.full((CHUNK, TILE), -1, I32)
    row = lax.broadcasted_iota(I32, (8, TILE), 1)
    for t in range(4):
        static = jnp.full((8, TILE), -1, I32)
        for q in range(7, 19):
            axes = [a for a in range(3) if VEL[q][a]]
            masks = [face_lanes(2 * a + (0 if VEL[q][a] < 0 else 1), t, row) for a in axes]
            if all(m is not None for m in masks):
                static = jnp.where(masks[0] & masks[1], static & ~(1 << BIT[q]), static)
        static = jnp.concatenate([static] * (CHUNK // 8), axis=0)
        below = yz[t - 1] if t > 0 else ones
        above = yz[t + 1] if t < 3 else ones
        up = roll(jnp.where(lane >= 64, below, yz[t]), 64) << 18
        down = roll(jnp.where(lane < 64, above, yz[t]), 64) & 511
        word = (up | (yz[t] << 9) | down) & static
        for d in range(6):
            m = face_lanes(d, t, lane)
            if m is not None:
                word = word & jnp.where(m, pw[d, rs, :], -1)
        code[rs, cols(t)] = word


def coarse_table(src, k, tiles):
    half = (lax.broadcasted_iota(I32, (8, TILE), 1) & 7) >> 1
    parts = []
    for quadrant in range(4):
        for c in range(2):
            vals = src[k, 8 * c : 8 * c + 8, :]
            wide = []
            for t in tiles:
                idx = half + (32 * (quadrant // 2) + 4 * (quadrant % 2) + 8 * t)
                got = jnp.take_along_axis(vals, idx, axis=1, mode="promise_in_bounds")
                wide.append(got)
            parts.append(jnp.concatenate(wide, axis=1))
    return split(jnp.concatenate(parts, axis=0))


def kernel(
    n,
    pops,
    coarse,
    nbr,
    itf,
    solid,
    out,
    f,
    pa,
    pb,
    packs,
    gh,
    g0,
    g1,
    gx,
    xs0,
    xr0,
    xs1,
    xr1,
    xl,
    cfv,
    nv,
    iv,
    sv,
    cs,
    cr,
    gc,
    code,
    pw,
    rm,
    keys,
    pyz,
    pxl,
    pxr,
    pc,
    ct,
    in_sem,
    send_sem,
    recv_sem,
):
    me = lax.axis_index("blk")
    peers = (lax.rem(me + n - 1, n), lax.rem(me + 1, n))
    has = (me > 0, me < n - 1)
    lane = lanes()
    barrier = pltpu.get_barrier_semaphore()

    def both(act):
        for k in range(2):
            pl.when(has[k])(functools.partial(act, k))

    def greet(k):
        pl.semaphore_signal(barrier, inc=1, device_id=(peers[k],), device_id_type=MESH)

    both(greet)

    def fetch(k, src, dst):
        c = pltpu.make_async_copy(src, dst, in_sem.at[k])
        c.start()
        return c

    def fetch_tiles(k, t, w=1):
        part = pl.ds(t * TILE, w * TILE)
        return fetch(k, pops.at[:, :, part], f.at[:, :, part])

    in_n = fetch(0, nbr, nv)
    in_i = fetch(1, itf, iv)
    in_c = fetch(2, coarse, cfv)
    in_s = fetch(3, solid, sv)
    in_3 = fetch_tiles(4, 3)
    in_0 = fetch_tiles(5, 0)
    in_m = fetch_tiles(6, 1, 2)

    def remote(sem, src, dst, k):
        return pltpu.make_async_remote_copy(
            src_ref=src,
            dst_ref=dst,
            send_sem=send_sem.at[sem],
            recv_sem=recv_sem.at[sem],
            device_id=(peers[k],),
            device_id_type=MESH,
        )

    def copy_a(k):
        return remote(k, xs0.at[k], xr0.at[k], k)

    def copy_b(k):
        return remote(2 + k, xs1.at[k], xr1.at[k], k)

    def copy_c():
        return remote(4, cs, cr, 0)

    def no_side(d):
        @pl.when(jnp.logical_not(has[1 - d]))
        def _():
            xr0[d] = jnp.zeros(xr0.shape[1:], F32)
            xr1[d] = jnp.zeros(xr1.shape[1:], F32)
            if d == 0:
                cr[...] = jnp.zeros(cr.shape, F32)

    for d in range(2):
        no_side(d)

    def first_collide(t):
        for rs in CHUNKS:
            post = relax_delta([f[q, rs, cols(t)] for q in range(19)])
            store_post(post, pa, packs, xs0, keys[rs, :], t, lane, rs)

    def second_collide(t):
        for n, rs in enumerate(CHUNKS):
            cur = stream(pa, gh.at[0], gx.at[0], code, t, lane, rs, have=have[t][n])
            store_post(relax_delta(cur), pb, packs, xl, keys[rs, :], t, lane, rs)

    have = [[{} for _ in CHUNKS] for _ in range(4)]

    def early(t, qs):
        for n, rs in enumerate(CHUNKS):
            qs = [q for q in qs if q not in have[t][n]]
            cur = stream(pa, gh.at[0], gx.at[0], code, t, lane, rs, qs=qs)
            have[t][n].update(zip(qs, cur))

    def finish(t):
        for rs in CHUNKS:
            cur = stream(pb, gh.at[1], gx.at[1], code, t, lane, rs)
            wet = (code[rs, cols(t)] & (1 << BIT[0])) != 0
            for q in range(19):
                out[q, rs, cols(t)] = jnp.where(wet, cur[q], f[q, rs, cols(t)])

    whole = lax.broadcasted_iota(I32, (BLK, TILE), 1)

    def gather_tile(t, sub, coarse=True):
        for h in range(2):
            src = jnp.concatenate([packs[5 * h + i, :, cols(t)] for i in range(5)], axis=1)
            got = jnp.dot(pyz[h], split(src), preferred_element_type=F32)
            first = face_lanes(3 + 2 * h, t, whole)
            for i in range(5):
                part = slice(TILE * i, TILE * (i + 1))
                a, b = got[:BLK, part], got[BLK:, part]
                if h == 0:
                    if coarse:
                        a = a + gc[sub, i, :, cols(t)]
                    ghosts = roll(jnp.where(first, a, b), 64)
                else:
                    ghosts = jnp.where(first, roll(a, 8), roll(b, -8))
                gh[sub, 5 * h + i, :, cols(t)] = ghosts

    def edge_stream(k, part):
        t = 3 if k == 1 else 0
        qs = OTHERS[k][part]
        for n, rs in enumerate(CHUNKS):
            cur = stream(
                pa, gh.at[0], None, code, t, lane, rs, qs=qs, have=have[t][n], alone=True
            )
            for s, tile in enumerate(pack_halves(cur, k, lane)):
                xs1[k, rs, cols((part.start or 0) // 2 + s)] = tile
            for q, v in zip(qs, cur):
                if VEL[q][0] == 0 and (k == 0 or q not in CROSS[2]):
                    have[t][n][q] = v

    def local_x(d, src):
        return jnp.dot(pxl[d], split(src[d]), preferred_element_type=F32)

    def take_a(d):
        pl.when(has[1 - d])(lambda: copy_a(d).wait_recv())
        far = jnp.dot(pxr[d], split(xr0[d]), preferred_element_type=F32)
        g0[d] = g0[d] + far
        for s in range(5):
            gx[0, d, s] = layer(g0, d, s, slice(None))

    def take_b(d):
        pl.when(has[1 - d])(lambda: copy_b(d).wait_recv())
        g1[d] = jnp.dot(pxr[d], split(xr1[d]), preferred_element_type=F32)
        ghosts = their_coarse(g0, ct) if d == 1 else None
        for rs in CHUNKS:
            vals = far_edge(pa, d, g0, g1, ghosts, lane, rs)
            for s in range(5):
                gx[1, d, s, rs, :] = vals[s]

    def join(d):
        near = local_x(d, xl)
        theirs = rm[d] != 0.0
        for s in range(5):
            tile = near[:, (s // 2) * TILE : (s // 2 + 1) * TILE]
            tile = roll(tile, 64) if s % 2 else tile
            gx[1, d, s] = jnp.where(theirs, gx[1, d, s], tile)

    def coarse_fine(k):
        got = jnp.dot(pc[...], coarse_table(cr, k, range(4)), preferred_element_type=F32)
        for i in range(5):
            gc[k, i] = got[BLK * i : BLK * (i + 1)]

    in_n.wait()
    in_i.wait()
    build_tables(me, nv, iv, pyz, pxl, pxr, pc, pw, rm, keys)
    in_c.wait()
    coarse_ghost(cfv, cs)
    in_s.wait()
    for rs in CHUNKS:
        build_code(sv, pw, code, lane, rs)
    in_3.wait()
    first_collide(3)
    gather_tile(3, 0, coarse=False)
    edge_stream(1, slice(None))
    pl.semaphore_wait(barrier, has[0].astype(I32) + has[1].astype(I32))
    pl.when(has[0])(lambda: copy_c().start())

    @pl.when(has[1])
    def _():
        copy_a(1).start()
        copy_b(1).start()

    in_0.wait()
    first_collide(0)
    pl.when(has[0])(lambda: copy_a(0).start())
    in_m.wait()
    first_collide(1)
    first_collide(2)
    ct[...] = coarse_table(cs, 0, (3,))
    for d in range(2):
        g0[d] = local_x(d, xs0)
    for t in range(3):
        gather_tile(t, 0, coarse=False)
    edge_stream(0, slice(0, 10))
    dry = [q for q in range(19) if q not in CROSS[2]]
    early(0, [q for q in dry if VEL[q][0] != 1])
    early(1, dry)
    early(2, dry)
    early(3, [q for q in dry if VEL[q][0] != -1])

    pl.when(has[1])(lambda: copy_c().wait_recv())
    coarse_fine(0)
    first = face_lanes(3, 0, lax.broadcasted_iota(I32, (BLK, 4 * TILE), 1))
    for i in range(5):
        gh[0, i] = jnp.where(first, gh[0, i] + gc[0, i], gh[0, i])
    edge_stream(0, slice(10, 14))
    pl.when(has[0])(lambda: copy_b(0).start())
    second_collide(1)
    second_collide(2)
    coarse_fine(1)

    def tail(near):
        far = 1 - near
        tile = {0: 3, 1: 0}
        mid = {0: 2, 1: 1}
        take_a(near)
        second_collide(tile[near])
        take_b(near)
        gather_tile(1, 1)
        gather_tile(2, 1)
        take_a(far)
        second_collide(tile[far])
        gather_tile(3, 1)
        gather_tile(0, 1)
        finish(mid[near])
        join(near)
        finish(tile[near])
        finish(mid[far])
        take_b(far)
        join(far)
        finish(tile[far])

    is_even = lax.rem(me, 2) == 0
    pl.when(is_even)(lambda: tail(0))
    pl.when(jnp.logical_not(is_even))(lambda: tail(1))

    def drain(k):
        copy_a(k).wait_send()
        copy_b(k).wait_send()
        if k == 0:
            copy_c().wait_send()

    both(drain)


def body(populations, coarse_faces, neighbors, interface, solid):
    n = lax.axis_size("blk")
    pops = jnp.transpose(populations, (1, 0, 2))
    coarse = jnp.transpose(coarse_faces, (0, 2, 1, 3))
    ins = (pops, coarse, neighbors.T, interface.T, solid)
    ins = [pltpu.with_memory_space_constraint(v, pltpu.HBM) for v in ins]
    anywhere = pl.BlockSpec(memory_space=pl.ANY)
    vm = pltpu.VMEM
    big = vm((19, BLK, 512), F32)
    done = pl.pallas_call(
        functools.partial(kernel, n),
        out_shape=jax.ShapeDtypeStruct((19, BLK, 512), F32),
        in_specs=[anywhere] * 5,
        out_specs=pl.BlockSpec(memory_space=pltpu.VMEM),
        scratch_shapes=[
            big,
            big,
            big,
            vm((10, BLK, 512), F32),
            vm((2, 10, BLK, 512), F32),
            vm((2, BLK, 384), F32),
            vm((2, BLK, 896), F32),
            vm((2, 2, 5, BLK, TILE), F32),
            vm((2, BLK, 384), F32),
            vm((2, BLK, 384), F32),
            vm((2, BLK, 896), F32),
            vm((2, BLK, 896), F32),
            vm((2, BLK, 384), F32),
            vm((2, 19, 2, 64), F32),
            vm((6, BLK), I32),
            vm((2, BLK), I32),
            vm((BLK, 512), I32),
            vm((2, 16, TILE), F32),
            vm((2, 16, TILE), F32),
            vm((2, 5, BLK, 512), F32),
            vm((BLK, 512), I32),
            vm((6, BLK, TILE), I32),
            vm((2, BLK, TILE), F32),
            vm((BLK, TILE), F32),
            vm((2, 2 * BLK, 2 * BLK), BF16),
            vm((2, BLK, 2 * BLK), BF16),
            vm((2, BLK, 2 * BLK), BF16),
            vm((5 * BLK, TILE), BF16),
            vm((TILE, TILE), BF16),
            pltpu.SemaphoreType.DMA((7,)),
            pltpu.SemaphoreType.DMA((5,)),
            pltpu.SemaphoreType.DMA((5,)),
        ],
        compiler_params=pltpu.CompilerParams(
            collective_id=0, has_side_effects=True, vmem_limit_bytes=40 * 2**20
        ),
    )(*ins)
    return jnp.transpose(done, (1, 0, 2))


def solution(mesh):
    placed = (
        P("blk", None, None),
        P("blk", None, None, None),
        P("blk", None),
        P("blk", None),
        P("blk", None),
    )
    return jax.shard_map(
        body, mesh=mesh, in_specs=placed, out_specs=P("blk", None, None), check_vma=False
    )
```

```python
import functools

import jax
import jax.numpy as jnp
import numpy as np
from jax import lax
from jax.experimental import pallas as pl
from jax.experimental.pallas import tpu as pltpu
from jax.sharding import PartitionSpec as P

MESH = pl.DeviceIdType.MESH
F32 = jnp.float32
BF16 = jnp.bfloat16
I32 = jnp.int32

VEL = [
    (0, 0, 0),
    (1, 0, 0),
    (-1, 0, 0),
    (0, 1, 0),
    (0, -1, 0),
    (0, 0, 1),
    (0, 0, -1),
    (1, 1, 0),
    (-1, -1, 0),
    (1, -1, 0),
    (-1, 1, 0),
    (1, 0, 1),
    (-1, 0, -1),
    (1, 0, -1),
    (-1, 0, 1),
    (0, 1, 1),
    (0, -1, -1),
    (0, 1, -1),
    (0, -1, 1),
]
OPP = [VEL.index((-x, -y, -z)) for x, y, z in VEL]
CROSS = [
    [q for q in range(19) if VEL[q][d // 2] == (-1 if d % 2 == 0 else 1)] for d in range(6)
]
BIT = [9 * (x + 1) + 3 * (y + 1) + (z + 1) for x, y, z in VEL]
OTHERS = [
    [q for q in range(19) if q not in CROSS[1 - d] and q not in CROSS[2]]
    + [q for q in CROSS[2] if q not in CROSS[1 - d]]
    for d in range(2)
]
BLK = 32
TILE = 128
CHUNK = 16
CHUNKS = [slice(r, r + CHUNK) for r in range(0, BLK, CHUNK)]


def relax_delta(f):
    s = 1.0 / 0.6
    sx, dx = f[1] + f[2], f[1] - f[2]
    sy, dy = f[3] + f[4], f[3] - f[4]
    sz, dz = f[5] + f[6], f[5] - f[6]
    s7, d7 = f[7] + f[8], f[7] - f[8]
    s9, d9 = f[9] + f[10], f[9] - f[10]
    s11, d11 = f[11] + f[12], f[11] - f[12]
    s13, d13 = f[13] + f[14], f[13] - f[14]
    s15, d15 = f[15] + f[16], f[15] - f[16]
    s17, d17 = f[17] + f[18], f[17] - f[18]
    sa, ta = s7 + s9, s7 - s9
    sb, tb = s11 + s13, s11 - s13
    sc, tc = s15 + s17, s15 - s17
    ax, ay = d7 + d9, d7 - d9
    bx, bz = d11 + d13, d11 - d13
    cy, cz = d15 + d17, d15 - d17
    x2, mx = ax + bx, ax - bx
    y2, my = ay + cy, cy - ay
    z2, mz = bz + cz, bz - cz
    jx, jy, jz = dx + x2, dy + y2, dz + z2
    ab = sa + sb
    s2 = ab + sc
    yz = sy + sz
    s1 = sx + yz
    rho = f[0] + (s1 + s2)
    inv = 1.0 / rho
    ux, uy, uz = jx * inv, jy * inv, jz * inv
    xx, yy, zz = jx * ux, jy * uy, jz * uz
    jj = (xx + yy) + zz
    m1 = (s2 - f[0]) - jj
    m2 = 9.0 * f[0] - 7.0 * s1 - 2.0 * s2 + 5.5 * jj
    c1 = m1 * (19.0 * 1.19 / 2394.0)
    c2 = m2 * (1.4 / 252.0)
    a9 = (sx + sx) - yz
    b9 = ab - (sc + sc)
    e9 = (xx + xx) - (yy + zz)
    c9 = (a9 + b9 - e9) * (s / 36.0)
    c10 = (b9 - 2.0 * a9 + 0.5 * e9) * (1.4 / 72.0)
    a11 = sy - sz
    b11 = sa - sb
    e11 = yy - zz
    c11 = (a11 + b11 - e11) * (s / 12.0)
    c12 = (b11 - 2.0 * a11 + 0.5 * e11) * (1.4 / 24.0)
    c13 = (ta - jx * uy) * (s / 4.0)
    c14 = (tc - jy * uz) * (s / 4.0)
    c15 = (tb - jx * uz) * (s / 4.0)
    g = (5.0 / 3.0) * 1.2 / 40.0
    c4 = (x2 - 2.0 * dx) * g
    c6 = (y2 - 2.0 * dy) * g
    c8 = (z2 - 2.0 * dz) * g
    h = 1.98 / 8.0
    c16, c17, c18 = mx * h, my * h, mz * h
    r0 = 12.0 * c2 - 30.0 * c1
    ra = -11.0 * c1 - 4.0 * c2
    rd = 8.0 * c1 + c2
    p9 = c9 - 2.0 * c10
    p11 = c11 - 2.0 * c12
    n9 = c9 + c10
    n11 = c11 + c12
    ex = ra + 2.0 * p9
    et = ra - p9
    ey, ez = et + p11, et - p11
    rt = rd + n9
    exy, exz = rt + n11, rt - n11
    eyz = rd - 2.0 * n9
    ox, oy, oz = -4.0 * c4, -4.0 * c6, -4.0 * c8
    xa, ya = c4 + c16, c6 - c17
    xb, zb = c4 - c16, c8 + c18
    yc, zc = c6 + c17, c8 - c18
    e7, e9_ = exy + c13, exy - c13
    e11_, e13 = exz + c15, exz - c15
    e15, e17 = eyz + c14, eyz - c14
    o7, o9 = xa + ya, xa - ya
    o11, o13 = xb + zb, xb - zb
    o15, o17 = yc + zc, yc - zc
    out = [f[0] - r0]
    for q, even, odd in (
        (1, ex, ox),
        (3, ey, oy),
        (5, ez, oz),
        (7, e7, o7),
        (9, e9_, o9),
        (11, e11_, o11),
        (13, e13, o13),
        (15, e15, o15),
        (17, e17, o17),
    ):
        out.append(f[q] - (even + odd))
        out.append(f[q + 1] - (even - odd))
    return out


def split(x):
    hi = x.astype(BF16)
    lo = (x - hi.astype(F32)).astype(BF16)
    return jnp.concatenate([hi, lo], axis=0)


def roll(x, by):
    by %= TILE
    return pltpu.roll(x, by, 1) if by else x


def lanes():
    return lax.broadcasted_iota(I32, (CHUNK, TILE), 1)


def face_lanes(d, t, lane):
    if d == 0:
        return lane >= 64 if t == 3 else None
    if d == 1:
        return lane < 64 if t == 0 else None
    pos = ((lane >> 3) & 7) if d < 4 else (lane & 7)
    return pos == (7 if d % 2 == 0 else 0)


def cols(t):
    return pl.ds(t * TILE, TILE)


def pack_halves(vals, d, lane):
    keep = lane < 64 if d == 0 else lane >= 64
    tiles = []
    for s in range(0, len(vals), 2):
        tiles.append(jnp.where(keep, vals[s], roll(vals[s + 1], 64)))
    return tiles


def layer(ref, d, n, rs):
    tile = ref[d, rs, cols(n // 2)]
    return roll(tile, 64) if n % 2 else tile


def store_post(post, ref, packs, xs, key, t, lane, rs):
    for q in range(19):
        ref[q, rs, cols(t)] = post[q]
    first = [face_lanes(3, t, lane), face_lanes(5, t, lane)]
    for h in range(2):
        for n in range(5):
            a, b = CROSS[2 + 2 * h][n], CROSS[3 + 2 * h][n]
            packs[5 * h + n, rs, cols(t)] = jnp.where(first[h], post[a], post[b])
    if t in (0, 3):
        d = 0 if t == 0 else 1
        vals = [post[q] for q in CROSS[d]] + [key]
        for s, tile in enumerate(pack_halves(vals, d, lane)):
            xs[d, rs, cols(s)] = tile


def stream(ref, gh, gx, code_ref, t, lane, rs, qs=tuple(range(19)), have=None, alone=False):
    post = [ref[q, rs, cols(t)] for q in range(19)]
    code = code_ref[rs, cols(t)]
    upper = lane >= 64

    def merged(ex, here, load, edge):
        if ex == 0 or alone:
            return here
        near = t - ex
        other = load(near) if 0 <= near <= 3 else edge
        if other is None:
            return here
        return jnp.where(upper, other, here) if ex == 1 else jnp.where(upper, here, other)

    out = []
    for q in qs:
        if have and q in have:
            out.append(have[q])
            continue
        if q == 0:
            out.append(post[0])
            continue
        ex, ey, ez = VEL[q]
        edge = None
        if not alone and not 0 <= t - ex <= 3:
            d = 0 if ex == -1 else 1
            edge = gx[d, CROSS[d].index(q), rs, :]
        src = merged(ex, post[q], lambda u: ref[q, rs, cols(u)], edge)

        def ghost(n, at):
            here = gh[n, rs, cols(t)]
            if ex == 0 or alone or not 0 <= t - ex <= 3:
                return here
            other = gh[n, rs, cols(t - ex)]
            return jnp.where(at, other, here) if ex == 1 else jnp.where(at, here, other)

        if ey:
            d = 2 if ey < 0 else 3
            g = ghost(CROSS[d].index(q), jnp.logical_not(upper))
            src = jnp.where(face_lanes(d ^ 1, t, lane), g, src)
        if ez:
            d = 4 if ez < 0 else 5
            wrapped = face_lanes(3 if ez < 0 else 2, t, lane)
            g = ghost(5 + CROSS[d].index(q), jnp.logical_xor(upper, wrapped))
            src = jnp.where(face_lanes(d ^ 1, t, lane), g, src)
        moved = roll(src, 64 * ex + 8 * ey + ez)
        usable = (code & (1 << BIT[q])) != 0
        out.append(jnp.where(usable, moved, post[OPP[q]]))
    return out


def far_edge(ref, d, g0, g1, ghosts, lane, rs):
    t = 3 if d == 0 else 0
    cur = [None] * 19
    for n, q in enumerate(OTHERS[d]):
        cur[q] = layer(g1, d, n, rs)
    for q in CROSS[1 - d]:
        ex, ey, ez = VEL[q]
        moved = roll(ref[q, rs, cols(t)], 64 + 8 * ey + ez)
        back = layer(g0, d, CROSS[d].index(OPP[q]), rs)
        for f, comp in ((2 if ey < 0 else 3, ey), (4 if ez < 0 else 5, ez)):
            if comp:
                moved = jnp.where(face_lanes(f, t, lane), back, moved)
        cur[q] = moved
    if d == 1:
        key = ghosts[0][rs]
        ghost = [g[rs] for g in ghosts[1]]
        for s, q in enumerate(CROSS[2]):
            ex, ey, ez = VEL[q]
            if ex < 0:
                continue
            at = face_lanes(2, 3, lane) & (key >= 0.0)
            if ez:
                at = at & jnp.logical_not(face_lanes(4 if ez < 0 else 5, 3, lane))
            cur[q] = jnp.where(at, roll(ghost[s], ez), cur[q])
    post = relax_delta(cur)
    return [post[q] for q in CROSS[d]]


def their_coarse(g0, ct):
    tile = g0[1, :, cols(2)]
    lane = lax.broadcasted_iota(I32, (BLK, TILE), 1)
    key = jnp.where(lane >= 64, roll(tile, 64), tile)
    out = jnp.dot(coarse_pick(key, lane), ct[...], preferred_element_type=F32)
    return key, [out[BLK * n : BLK * (n + 1)] for n in range(5)]


def coarse_pick(key, lane):
    group = ((lane & 63) >> 3).astype(F32)
    mine = key == group
    rows = [jnp.where(mine & ((lane & 7) == n), 1.0, 0.0) for n in range(5)]
    return jnp.concatenate(rows, axis=0).astype(BF16)


def coarse_ghost(cfv, cs):
    ratio = 0.6 / 1.1
    cs[...] = jnp.zeros((2, 16, TILE), F32)
    row = lax.broadcasted_iota(I32, (2, 64), 0)
    w0 = jnp.where(row == 0, 0.0, 0.5)
    w1 = jnp.where(row == 0, 1.0, 0.5)

    def total(items):
        return functools.reduce(lambda a, b: a + b, items)

    for c in range(2):
        hs = []
        for q in range(19):
            both = cfv[c, q, :, :]
            hs.append(w1 * both + w0 * both[0:1, :])
        rho = total(hs)
        inv = 1.0 / rho
        vel = []
        for axis in range(3):
            plus = total([hs[q] for q in range(19) if VEL[q][axis] == 1])
            minus = total([hs[q] for q in range(19) if VEL[q][axis] == -1])
            vel.append((plus - minus) * inv)
        sq = 1.0 - 1.5 * (vel[0] * vel[0] + vel[1] * vel[1] + vel[2] * vel[2])
        for s, q in enumerate(CROSS[2]):
            proj = total(
                [v if e == 1 else -v for v, e in zip(vel, VEL[q]) if e]
            )
            weight = 1.0 / 18.0 if q < 7 else 1.0 / 36.0
            eq = (weight * rho) * (sq + 3.0 * proj + 4.5 * proj * proj)
            val = eq + ratio * (hs[q] - eq)
            for k in range(2):
                cs[k, pl.ds(8 * c + s, 1), 0:64] = val[k : k + 1, :]


def build_tables(me, nv, iv, pyz, pxl, pxr, pc, pw, rm, keys):
    row, col = (lax.broadcasted_iota(I32, (BLK, BLK), a) for a in (0, 1))
    eye = row == col

    def column(vals):
        wide = jnp.broadcast_to(vals.astype(F32), (BLK, BLK))
        return jnp.sum(jnp.where(eye, wide, 0.0), axis=1, keepdims=True)

    face = [column(nv[d : d + 1, :]) for d in range(6)]
    cb = column(iv[0:1, :])
    quad = column(iv[1:2, :])
    first = (me * BLK).astype(F32)
    slot = (lax.broadcasted_iota(I32, (BLK, 2 * BLK), 1) & (BLK - 1)).astype(F32)
    for d in range(6):
        local = jnp.where(face[d] >= 0.0, face[d] - first, -1.0)
        one = jnp.where(local == slot, 1.0, 0.0).astype(BF16)
        if d < 2:
            pxl[d] = one
            shift = -float(BLK) if d == 0 else float(BLK)
            there = jnp.where(face[d] >= 0.0, face[d] - first + shift, -1.0)
            pxr[d] = jnp.where(there == slot, 1.0, 0.0).astype(BF16)
            mine = (there >= 0.0) & (there < float(BLK))
            rm[d] = jnp.broadcast_to(jnp.where(mine, 1.0, 0.0), (BLK, TILE))
        else:
            pyz[d // 2 - 1, BLK * (d % 2) : BLK * (d % 2 + 1)] = one
    key = jnp.where(cb >= 0.0, 2.0 * quad + cb - 2.0 * (me + 1).astype(F32), -1.0)
    keys[...] = jnp.broadcast_to(key, (BLK, TILE))
    pc[...] = coarse_pick(key, lax.broadcasted_iota(I32, (BLK, TILE), 1))
    for d in range(6):
        there = face[d] >= 0.0
        if d == 2:
            there = there | (cb >= 0.0)
        bits = sum(1 << BIT[q] for q in CROSS[d])
        pw[d] = jnp.broadcast_to(jnp.where(there, -1, ~bits), (BLK, TILE))


def build_code(sv, pw, code, lane, rs):
    yz = []
    for t in range(4):
        fl = 1 - sv[rs, cols(t)]
        wz = roll(fl, -1) | (fl << 1) | (roll(fl, 1) << 2)
        yz.append(roll(wz, -8) | (wz << 3) | (roll(wz, 8) << 6))
    ones = jnp.full((CHUNK, TILE), -1, I32)
    row = lax.broadcasted_iota(I32, (8, TILE), 1)
    for t in range(4):
        static = jnp.full((8, TILE), -1, I32)
        for q in range(7, 19):
            axes = [a for a in range(3) if VEL[q][a]]
            masks = [face_lanes(2 * a + (0 if VEL[q][a] < 0 else 1), t, row) for a in axes]
            if all(m is not None for m in masks):
                static = jnp.where(masks[0] & masks[1], static & ~(1 << BIT[q]), static)
        static = jnp.concatenate([static] * (CHUNK // 8), axis=0)
        below = yz[t - 1] if t > 0 else ones
        above = yz[t + 1] if t < 3 else ones
        up = roll(jnp.where(lane >= 64, below, yz[t]), 64) << 18
        down = roll(jnp.where(lane < 64, above, yz[t]), 64) & 511
        word = (up | (yz[t] << 9) | down) & static
        for d in range(6):
            m = face_lanes(d, t, lane)
            if m is not None:
                word = word & jnp.where(m, pw[d, rs, :], -1)
        code[rs, cols(t)] = word


def coarse_table(src, k, tiles):
    half = (lax.broadcasted_iota(I32, (8, TILE), 1) & 7) >> 1
    parts = []
    for quadrant in range(4):
        for c in range(2):
            vals = src[k, 8 * c : 8 * c + 8, :]
            wide = []
            for t in tiles:
                idx = half + (32 * (quadrant // 2) + 4 * (quadrant % 2) + 8 * t)
                got = jnp.take_along_axis(vals, idx, axis=1, mode="promise_in_bounds")
                wide.append(got)
            parts.append(jnp.concatenate(wide, axis=1))
    return split(jnp.concatenate(parts, axis=0))


def kernel(
    n,
    pops,
    coarse,
    nbr,
    itf,
    solid,
    out,
    f,
    pa,
    pb,
    packs,
    gh,
    g0,
    g1,
    gx,
    xs0,
    xr0,
    xs1,
    xr1,
    xl,
    cfv,
    nv,
    iv,
    sv,
    cs,
    cr,
    gc,
    code,
    pw,
    rm,
    keys,
    pyz,
    pxl,
    pxr,
    pc,
    ct,
    in_sem,
    send_sem,
    recv_sem,
):
    me = lax.axis_index("blk")
    peers = (lax.rem(me + n - 1, n), lax.rem(me + 1, n))
    has = (me > 0, me < n - 1)
    lane = lanes()
    barrier = pltpu.get_barrier_semaphore()

    def both(act):
        for k in range(2):
            pl.when(has[k])(functools.partial(act, k))

    def greet(k):
        pl.semaphore_signal(barrier, inc=1, device_id=(peers[k],), device_id_type=MESH)

    both(greet)

    def fetch(k, src, dst):
        c = pltpu.make_async_copy(src, dst, in_sem.at[k])
        c.start()
        return c

    def fetch_tiles(k, t, w=1):
        part = pl.ds(t * TILE, w * TILE)
        return fetch(k, pops.at[:, :, part], f.at[:, :, part])

    in_n = fetch(0, nbr, nv)
    in_i = fetch(1, itf, iv)
    in_c = fetch(2, coarse, cfv)
    in_s = fetch(3, solid, sv)
    in_3 = fetch_tiles(4, 3)
    in_0 = fetch_tiles(5, 0)
    in_m = fetch_tiles(6, 1, 2)

    def remote(sem, src, dst, k):
        return pltpu.make_async_remote_copy(
            src_ref=src,
            dst_ref=dst,
            send_sem=send_sem.at[sem],
            recv_sem=recv_sem.at[sem],
            device_id=(peers[k],),
            device_id_type=MESH,
        )

    def copy_a(k):
        return remote(k, xs0.at[k], xr0.at[k], k)

    def copy_b(k):
        return remote(2 + k, xs1.at[k], xr1.at[k], k)

    def copy_c():
        return remote(4, cs, cr, 0)

    def no_side(d):
        @pl.when(jnp.logical_not(has[1 - d]))
        def _():
            xr0[d] = jnp.zeros(xr0.shape[1:], F32)
            xr1[d] = jnp.zeros(xr1.shape[1:], F32)
            if d == 0:
                cr[...] = jnp.zeros(cr.shape, F32)

    for d in range(2):
        no_side(d)

    def first_collide(t):
        for rs in CHUNKS:
            post = relax_delta([f[q, rs, cols(t)] for q in range(19)])
            store_post(post, pa, packs, xs0, keys[rs, :], t, lane, rs)

    def second_collide(t):
        for n, rs in enumerate(CHUNKS):
            cur = stream(pa, gh.at[0], gx.at[0], code, t, lane, rs, have=have[t][n])
            store_post(relax_delta(cur), pb, packs, xl, keys[rs, :], t, lane, rs)

    have = [[{} for _ in CHUNKS] for _ in range(4)]

    def early(t, qs):
        for n, rs in enumerate(CHUNKS):
            qs = [q for q in qs if q not in have[t][n]]
            cur = stream(pa, gh.at[0], gx.at[0], code, t, lane, rs, qs=qs)
            have[t][n].update(zip(qs, cur))

    def finish(t):
        for rs in CHUNKS:
            cur = stream(pb, gh.at[1], gx.at[1], code, t, lane, rs)
            wet = (code[rs, cols(t)] & (1 << BIT[0])) != 0
            for q in range(19):
                out[q, rs, cols(t)] = jnp.where(wet, cur[q], f[q, rs, cols(t)])

    whole = lax.broadcasted_iota(I32, (BLK, TILE), 1)

    def gather_tile(t, sub, coarse=True):
        for h in range(2):
            src = jnp.concatenate([packs[5 * h + i, :, cols(t)] for i in range(5)], axis=1)
            got = jnp.dot(pyz[h], split(src), preferred_element_type=F32)
            first = face_lanes(3 + 2 * h, t, whole)
            for i in range(5):
                part = slice(TILE * i, TILE * (i + 1))
                a, b = got[:BLK, part], got[BLK:, part]
                if h == 0:
                    if coarse:
                        a = a + gc[sub, i, :, cols(t)]
                    ghosts = roll(jnp.where(first, a, b), 64)
                else:
                    ghosts = jnp.where(first, roll(a, 8), roll(b, -8))
                gh[sub, 5 * h + i, :, cols(t)] = ghosts

    def edge_stream(k, part):
        t = 3 if k == 1 else 0
        qs = OTHERS[k][part]
        for n, rs in enumerate(CHUNKS):
            cur = stream(
                pa, gh.at[0], None, code, t, lane, rs, qs=qs, have=have[t][n], alone=True
            )
            for s, tile in enumerate(pack_halves(cur, k, lane)):
                xs1[k, rs, cols((part.start or 0) // 2 + s)] = tile
            for q, v in zip(qs, cur):
                if VEL[q][0] == 0 and (k == 0 or q not in CROSS[2]):
                    have[t][n][q] = v

    def local_x(d, src):
        return jnp.dot(pxl[d], split(src[d]), preferred_element_type=F32)

    def take_a(d):
        pl.when(has[1 - d])(lambda: copy_a(d).wait_recv())
        far = jnp.dot(pxr[d], split(xr0[d]), preferred_element_type=F32)
        g0[d] = g0[d] + far
        for s in range(5):
            gx[0, d, s] = layer(g0, d, s, slice(None))

    def take_b(d):
        pl.when(has[1 - d])(lambda: copy_b(d).wait_recv())
        g1[d] = jnp.dot(pxr[d], split(xr1[d]), preferred_element_type=F32)
        ghosts = their_coarse(g0, ct) if d == 1 else None
        for rs in CHUNKS:
            vals = far_edge(pa, d, g0, g1, ghosts, lane, rs)
            for s in range(5):
                gx[1, d, s, rs, :] = vals[s]

    def join(d):
        near = local_x(d, xl)
        theirs = rm[d] != 0.0
        for s in range(5):
            tile = near[:, (s // 2) * TILE : (s // 2 + 1) * TILE]
            tile = roll(tile, 64) if s % 2 else tile
            gx[1, d, s] = jnp.where(theirs, gx[1, d, s], tile)

    def coarse_fine(k):
        got = jnp.dot(pc[...], coarse_table(cr, k, range(4)), preferred_element_type=F32)
        for i in range(5):
            gc[k, i] = got[BLK * i : BLK * (i + 1)]

    in_n.wait()
    in_i.wait()
    build_tables(me, nv, iv, pyz, pxl, pxr, pc, pw, rm, keys)
    in_c.wait()
    coarse_ghost(cfv, cs)
    in_s.wait()
    for rs in CHUNKS:
        build_code(sv, pw, code, lane, rs)
    in_3.wait()
    first_collide(3)
    gather_tile(3, 0, coarse=False)
    edge_stream(1, slice(None))

    @pl.when(me == 0)
    def _():
        pl.semaphore_wait(barrier, 1)
        copy_a(1).start()
        copy_b(1).start()

    in_0.wait()
    first_collide(0)
    in_m.wait()
    first_collide(1)
    first_collide(2)
    ct[...] = coarse_table(cs, 0, (3,))
    for d in range(2):
        g0[d] = local_x(d, xs0)
    for t in range(3):
        gather_tile(t, 0, coarse=False)
    edge_stream(0, slice(0, 10))
    dry = [q for q in range(19) if q not in CROSS[2]]
    early(0, [q for q in dry if VEL[q][0] != 1])
    early(1, dry)
    early(2, dry)
    early(3, [q for q in dry if VEL[q][0] != -1])

    @pl.when(me > 0)
    def _():
        pl.semaphore_wait(barrier, 1 + has[1].astype(I32))
        copy_c().start()

        @pl.when(has[1])
        def _():
            copy_a(1).start()
            copy_b(1).start()

        copy_a(0).start()

    odd = lax.rem(me, 2) == 1

    def take_near():
        take_a(1)
        take_b(1)

    pl.when(odd & (me != 1))(take_near)
    pl.when(has[1])(lambda: copy_c().wait_recv())
    coarse_fine(0)
    first = face_lanes(3, 0, lax.broadcasted_iota(I32, (BLK, 4 * TILE), 1))
    for i in range(5):
        gh[0, i] = jnp.where(first, gh[0, i] + gc[0, i], gh[0, i])
    edge_stream(0, slice(10, 14))
    pl.when(has[0])(lambda: copy_b(0).start())
    second_collide(1)
    second_collide(2)
    coarse_fine(1)

    def tail(near):
        far = 1 - near
        tile = {0: 3, 1: 0}
        mid = {0: 2, 1: 1}
        if near == 0:
            take_a(near)
            second_collide(tile[near])
            take_b(near)
        else:
            pl.when(me == 1)(take_near)
            second_collide(tile[near])
        gather_tile(1, 1)
        gather_tile(2, 1)
        take_a(far)
        second_collide(tile[far])
        gather_tile(3, 1)
        gather_tile(0, 1)
        finish(mid[near])
        join(near)
        finish(tile[near])
        finish(mid[far])
        take_b(far)
        join(far)
        finish(tile[far])

    pl.when(jnp.logical_not(odd))(lambda: tail(0))
    pl.when(odd)(lambda: tail(1))

    def drain(k):
        copy_a(k).wait_send()
        copy_b(k).wait_send()
        if k == 0:
            copy_c().wait_send()

    both(drain)


def body(populations, coarse_faces, neighbors, interface, solid):
    n = lax.axis_size("blk")
    pops = jnp.transpose(populations, (1, 0, 2))
    coarse = jnp.transpose(coarse_faces, (0, 2, 1, 3))
    ins = (pops, coarse, neighbors.T, interface.T, solid)
    ins = [pltpu.with_memory_space_constraint(v, pltpu.HBM) for v in ins]
    anywhere = pl.BlockSpec(memory_space=pl.ANY)
    vm = pltpu.VMEM
    big = vm((19, BLK, 512), F32)
    done = pl.pallas_call(
        functools.partial(kernel, n),
        out_shape=jax.ShapeDtypeStruct((19, BLK, 512), F32),
        in_specs=[anywhere] * 5,
        out_specs=pl.BlockSpec(memory_space=pltpu.VMEM),
        scratch_shapes=[
            big,
            big,
            big,
            vm((10, BLK, 512), F32),
            vm((2, 10, BLK, 512), F32),
            vm((2, BLK, 384), F32),
            vm((2, BLK, 896), F32),
            vm((2, 2, 5, BLK, TILE), F32),
            vm((2, BLK, 384), F32),
            vm((2, BLK, 384), F32),
            vm((2, BLK, 896), F32),
            vm((2, BLK, 896), F32),
            vm((2, BLK, 384), F32),
            vm((2, 19, 2, 64), F32),
            vm((6, BLK), I32),
            vm((2, BLK), I32),
            vm((BLK, 512), I32),
            vm((2, 16, TILE), F32),
            vm((2, 16, TILE), F32),
            vm((2, 5, BLK, 512), F32),
            vm((BLK, 512), I32),
            vm((6, BLK, TILE), I32),
            vm((2, BLK, TILE), F32),
            vm((BLK, TILE), F32),
            vm((2, 2 * BLK, 2 * BLK), BF16),
            vm((2, BLK, 2 * BLK), BF16),
            vm((2, BLK, 2 * BLK), BF16),
            vm((5 * BLK, TILE), BF16),
            vm((TILE, TILE), BF16),
            pltpu.SemaphoreType.DMA((7,)),
            pltpu.SemaphoreType.DMA((5,)),
            pltpu.SemaphoreType.DMA((5,)),
        ],
        compiler_params=pltpu.CompilerParams(
            collective_id=0, has_side_effects=True, vmem_limit_bytes=40 * 2**20
        ),
    )(*ins)
    return jnp.transpose(done, (1, 0, 2))


def solution(mesh):
    placed = (
        P("blk", None, None),
        P("blk", None, None, None),
        P("blk", None),
        P("blk", None),
        P("blk", None),
    )
    return jax.shard_map(
        body, mesh=mesh, in_specs=placed, out_specs=P("blk", None, None), check_vma=False
    )
```
